512 devices in a mesh: band: 128 (over z, y, core), chan: 4 (over x).
Axes of the slice: x: 4, y: 8, z: 8, core: 2. Of those that a mesh axis runs over, the one named last changes fastest.
Arguments:
- grid_state: bfloat16 [65536, 227], P('band'), may hold values from -8 to 8
- mesh_latent: bfloat16 [32768, 512], P('band', 'chan'), may hold values from -6 to 6
- w_in: bfloat16 [227, 512], P(None, 'chan'), may hold values from -0.375 to 0.375
- w_enc_src: bfloat16 [512, 512], P(None, 'chan'), may hold values from -0.25 to 0.25
- w_enc_dst: bfloat16 [512, 512], P(None, 'chan'), may hold values from -0.25 to 0.25
- w_enc_out: bfloat16 [512, 512], P(None, 'chan'), may hold values from -0.25 to 0.25
- w_proc: bfloat16 [2, 3, 512, 512], P(None, None, None, 'chan'), may hold values from -0.25 to 0.25
- w_dec_src: bfloat16 [512, 512], P(None, 'chan'), may hold values from -0.25 to 0.25
- w_dec_dst: bfloat16 [512, 512], P(None, 'chan'), may hold values from -0.25 to 0.25
- w_out: bfloat16 [512, 227], P('chan'), may hold values from -0.25 to 0.25
- enc_src: int32 [640, 512], P('band'), may hold values from 0 to 511
- enc_dst: int32 [640, 512], P('band'), may hold values from -1 to 255, as said below
- local_src: int32 [128, 1024], P('band'), may hold values from 0 to 255
- local_dst: int32 [128, 1024], P('band'), may hold values from 0 to 255
- proc_src: int32 [640, 128], P('band'), may hold values from 0 to 255
- proc_dst: int32 [640, 128], P('band'), may hold values from -1 to 255, as said below
- dec_src: int32 [640, 512], P('band'), may hold values from 0 to 255
- dec_dst: int32 [640, 512], P('band'), may hold values from -1 to 511, as said below
Outputs:
- increment: bfloat16 [65536, 227], P('band')
The draws below stay inside these ranges and needn't reach their ends.
Inputs may be any that keep to these rules, and one draw needn't show every extreme that they name: `enc_dst`: row a * 5 + j lists the grid-to-mesh edges from band a to partition (a + j - 2) mod 128; the filled slots of a row come first, the others hold -1; every row fills at least a quarter of its slots. `proc_dst`: row a * 5 + j lists the mesh edges from partition a to partition (a + j - 2) mod 128; the filled slots of a row come first, the others hold -1; every row fills at least a quarter of its slots. `dec_dst`: row a * 5 + j lists the mesh-to-grid edges from partition a to band (a + j - 2) mod 128; the filled slots of a row come first, the others hold -1; every row fills at least a quarter of its slots.
All inputs are finite; a program needn't handle non-finite values.
Results may differ from the reference program's by a relative error of at most 0.015.
Values may be sent and summed in bfloat16 or wider, within the bound.
No kernel may reach another device: no remote copies, remote signals or barrier semaphores. Data moves between devices by JAX's collectives and lax.ppermute only.
A program may use at most 64 MiB of HBM per device.

```python
import math
import jax
import jax.numpy as jnp
from jax import lax

C = 227
L = 512
LAYERS = 2
NEIGH = 5
G_DEV = 512
M_DEV = 256
GRID = 65536
MESH = 32768
BLOCKS = 640
CAP_E = 512
CAP_P = 128
CAP_D = 512
E_LOC = 1024
N_BAND = 128


def fill_blocks(key, capacity, targets):
    key_counts, key_heavy, key_values = jax.random.split(key, 3)
    counts = jax.random.randint(key_counts, (N_BAND, NEIGH), capacity // 4, capacity + 1)
    heavy_target = jax.random.randint(key_heavy, (), 0, N_BAND)
    receivers = (jnp.arange(N_BAND, dtype=jnp.int32)[:, None] + jnp.arange(NEIGH, dtype=jnp.int32)[None, :] - NEIGH // 2 + N_BAND) % N_BAND
    counts = jnp.where(receivers == heavy_target, capacity, counts)
    slot_ids = jnp.arange(capacity, dtype=jnp.int32)[None, None, :]
    filled = slot_ids < counts[:, :, None]
    values = jax.random.randint(key_values, (N_BAND, NEIGH, capacity), 0, targets)
    return jnp.where(filled, values, -1).reshape(N_BAND * NEIGH, capacity).astype(jnp.int32)


def draw_enc_dst(key, part):
    key = jax.random.fold_in(key, 11)
    return fill_blocks(key, CAP_E, M_DEV)


def draw_proc_dst(key, part):
    key = jax.random.fold_in(key, 12)
    return fill_blocks(key, CAP_P, M_DEV)


def draw_dec_dst(key, part):
    key = jax.random.fold_in(key, 13)
    return fill_blocks(key, CAP_D, G_DEV)


def draw_grid_state(key, part):
    key = jax.random.fold_in(key, 21)
    key_rows, key_cols, key_values = jax.random.split(key, 3)
    row_scale = jnp.exp(jax.random.uniform(key_rows, (GRID, 1), jnp.float32, math.log(0.3), math.log(3.0)))
    col_scale = jnp.exp(jax.random.uniform(key_cols, (1, C), jnp.float32, math.log(0.3), math.log(3.0)))
    values = jax.random.normal(key_values, (GRID, C), jnp.float32)
    return jnp.clip(values * row_scale * col_scale, -8.0, 8.0).astype(jnp.bfloat16)


def plant(entries, key, low, top_value):
    shape = entries.shape
    place = [jax.random.randint(jax.random.fold_in(key, axis), (), 0, shape[axis]) for axis in range(len(shape))]
    entries = entries.at[tuple(place)].set(low)
    longest = shape.index(max(shape))
    place[longest] = (place[longest] + 1) % shape[longest]
    return entries.at[tuple(place)].set(top_value)


def steps_of(rng, dims, pieces, smallest, high):
    gain, own = 1.0, jax.random.fold_in(rng, 6)
    for dim, blocks in pieces:
        steps = jnp.exp(jax.random.uniform(jax.random.fold_in(own, dim), (blocks,), jnp.float32, smallest / len(pieces), high / len(pieces)))
        gain = gain * jnp.repeat(steps, dims[dim] // blocks).reshape([-1 if axis == dim else 1 for axis in range(len(dims))])
    return gain


def bell_draw(own_key, dims, spread, bound, pieces=(), kind=jnp.bfloat16):
    array = jax.random.normal(own_key, dims, jnp.float32) * spread
    if len(pieces) > 0:
        array = steps_of(own_key, dims, pieces, -0.22, 0.18) * array
    return jnp.clip(array, min=-bound, max=bound).astype(kind)


def setup_inputs(seed: int = 0) -> dict:
    key_of = jax.random.split(jax.random.key(seed), 19)
    return {
        "grid_state": draw_grid_state(jax.random.fold_in(key_of[18], 71), 0),
        "mesh_latent": bell_draw(key_of[1], (MESH, L), 1.0, 6.0, ((0, 128), (1, 4))),
        "w_in": bell_draw(key_of[2], (C, L), C ** -0.5, 0.375, ((1, 4),)),
        "w_enc_src": bell_draw(key_of[3], (L, L), L ** -0.5, 0.25, ((1, 4),)),
        "w_enc_dst": bell_draw(key_of[4], (L, L), L ** -0.5, 0.25, ((1, 4),)),
        "w_enc_out": bell_draw(key_of[5], (L, L), L ** -0.5, 0.25, ((1, 4),)),
        "w_proc": bell_draw(key_of[6], (LAYERS, 3, L, L), L ** -0.5, 0.25, ((3, 4),)),
        "w_dec_src": bell_draw(key_of[7], (L, L), L ** -0.5, 0.25, ((1, 4),)),
        "w_dec_dst": bell_draw(key_of[8], (L, L), L ** -0.5, 0.25, ((1, 4),)),
        "w_out": bell_draw(key_of[9], (L, C), L ** -0.5, 0.25, ((0, 4),)),
        "enc_src": plant(jax.random.randint(key_of[10], (BLOCKS, CAP_E), 0, G_DEV), jax.random.fold_in(key_of[10], 1), 0, G_DEV - 1).astype(jnp.int32),
        "enc_dst": draw_enc_dst(jax.random.fold_in(key_of[18], 71), 0),
        "local_src": plant(jax.random.randint(key_of[12], (N_BAND, E_LOC), 0, M_DEV), jax.random.fold_in(key_of[12], 1), 0, M_DEV - 1).astype(jnp.int32),
        "local_dst": plant(jax.random.randint(key_of[13], (N_BAND, E_LOC), 0, M_DEV), jax.random.fold_in(key_of[13], 1), 0, M_DEV - 1).astype(jnp.int32),
        "proc_src": plant(jax.random.randint(key_of[14], (BLOCKS, CAP_P), 0, M_DEV), jax.random.fold_in(key_of[14], 1), 0, M_DEV - 1).astype(jnp.int32),
        "proc_dst": draw_proc_dst(jax.random.fold_in(key_of[18], 71), 0),
        "dec_src": plant(jax.random.randint(key_of[16], (BLOCKS, CAP_D), 0, M_DEV), jax.random.fold_in(key_of[16], 1), 0, M_DEV - 1).astype(jnp.int32),
        "dec_dst": draw_dec_dst(jax.random.fold_in(key_of[18], 71), 0),
    }


EPS = 1e-05

def normalize(values):
    values = values.astype(jnp.float32)
    return values * lax.rsqrt(lax.optimization_barrier(jnp.mean(values * values, axis=-1, keepdims=True)) + EPS)

def stored(values):
    return lax.optimization_barrier(values.astype(jnp.bfloat16))

def project(row_block, weight):
    return jnp.dot(row_block, weight, preferred_element_type=jnp.float32)

def route(sent_rows, sources, targets, send_count, recv_count, receiver):
    center = NEIGH // 2

    def collect_one(part):
        slots = jnp.arange(NEIGH, dtype=jnp.int32)
        senders = ((part - (slots - center) + N_BAND) % N_BAND).astype(jnp.int32)
        row_ids = (senders * NEIGH + slots).astype(jnp.int32)
        src_ids = jnp.take(sources, row_ids, axis=0)
        dst_ids = jnp.take(targets, row_ids, axis=0)
        global_src = (senders[:, None] * send_count + src_ids).reshape(-1).astype(jnp.int32)
        segment_ids = jnp.where(dst_ids < 0, recv_count, dst_ids).reshape(-1).astype(jnp.int32)
        own_recv = lax.dynamic_slice_in_dim(receiver, (part * recv_count).astype(jnp.int32), recv_count, 0)
        picked = jnp.take(own_recv, jnp.minimum(segment_ids, recv_count - 1), axis=0)
        message = jax.nn.silu(jnp.take(sent_rows, global_src, axis=0).astype(jnp.float32) + picked.astype(jnp.float32))
        return jax.ops.segment_sum(message, segment_ids, num_segments=recv_count + 1)[:recv_count]
    totals = lax.map(collect_one, jnp.arange(N_BAND, dtype=jnp.int32))
    return totals.reshape(N_BAND * recv_count, sent_rows.shape[1])

def inside_edges(sent_rows, receiver, sources, targets):

    def inside_one(part):
        src_ids = jnp.take(sources, part, axis=0).astype(jnp.int32)
        dst_ids = jnp.take(targets, part, axis=0).astype(jnp.int32)
        start = (part * M_DEV).astype(jnp.int32)
        own_send = lax.dynamic_slice_in_dim(sent_rows, start, M_DEV, 0)
        own_recv = lax.dynamic_slice_in_dim(receiver, start, M_DEV, 0)
        message = jax.nn.silu(jnp.take(own_send, src_ids, axis=0).astype(jnp.float32) + jnp.take(own_recv, dst_ids, axis=0).astype(jnp.float32))
        return jax.ops.segment_sum(message, dst_ids, num_segments=M_DEV)
    totals = lax.map(inside_one, jnp.arange(N_BAND, dtype=jnp.int32))
    return totals.reshape(N_BAND * M_DEV, sent_rows.shape[1])

def reference(grid_state, mesh_latent, w_in, w_enc_src, w_enc_dst, w_enc_out, w_proc, w_dec_src, w_dec_dst, w_out, enc_src, enc_dst, local_src, local_dst, proc_src, proc_dst, dec_src, dec_dst):
    grid_latent = stored(jax.nn.silu(project(grid_state, w_in)))
    grid_normed = normalize(grid_latent).astype(jnp.bfloat16)
    enc_send = project(grid_normed, w_enc_src).astype(jnp.bfloat16)
    mesh_normed = normalize(mesh_latent).astype(jnp.bfloat16)
    enc_recv = project(mesh_normed, w_enc_dst).astype(jnp.bfloat16)
    enc_agg = stored(route(enc_send, enc_src, enc_dst, G_DEV, M_DEV, enc_recv))
    mesh_state = mesh_latent.astype(jnp.float32) + project(normalize(enc_agg).astype(jnp.bfloat16), w_enc_out)
    for layer_index in range(LAYERS):
        mesh_rounded = stored(mesh_state)
        proc_normed = normalize(mesh_rounded).astype(jnp.bfloat16)
        proc_send = project(proc_normed, w_proc[layer_index, 0]).astype(jnp.bfloat16)
        proc_recv = project(proc_normed, w_proc[layer_index, 1]).astype(jnp.bfloat16)
        remote = route(proc_send, proc_src, proc_dst, M_DEV, M_DEV, proc_recv)
        inside = inside_edges(proc_send, proc_recv, local_src, local_dst)
        proc_agg = stored(remote + inside)
        mesh_state = mesh_state + project(normalize(proc_agg).astype(jnp.bfloat16), w_proc[layer_index, 2])
    mesh_rounded = stored(mesh_state)
    dec_normed = normalize(mesh_rounded).astype(jnp.bfloat16)
    dec_send = project(dec_normed, w_dec_src).astype(jnp.bfloat16)
    dec_recv = project(grid_normed, w_dec_dst).astype(jnp.bfloat16)
    dec_agg = stored(route(dec_send, dec_src, dec_dst, M_DEV, G_DEV, dec_recv))
    combined = dec_agg.astype(jnp.float32) + grid_latent.astype(jnp.float32)
    combined_normed = normalize(combined).astype(jnp.bfloat16)
    return project(combined_normed, w_out).astype(jnp.bfloat16)
```

```python
import jax
import jax.numpy as jnp
from jax import lax
from jax.experimental import pallas as pl
from jax.experimental.pallas import tpu as pltpu
from jax.sharding import Mesh, PartitionSpec as P

EPS = 1e-05
F32 = jnp.float32
BF16 = jnp.bfloat16
I32 = jnp.int32
LANES = 128
TILE = 32
TABLES = 5


def rms(values):
    values = values.astype(F32)
    return values * lax.rsqrt(jnp.mean(values * values, axis=-1, keepdims=True) + EPS)


def silu(values):
    return 0.5 * values * (1.0 + jnp.tanh(0.5 * values))


def dot(a, b):
    return lax.dot_general(a, b, (((1,), (0,)), ((), ())), preferred_element_type=F32)


def dot_first(a, b):
    return lax.dot_general(a, b, (((0,), (0,)), ((), ())), preferred_element_type=F32)


def dot_last(a, b):
    return lax.dot_general(a, b, (((1,), (1,)), ((), ())), preferred_element_type=F32)


def wide(ref, start, size):
    return jnp.concatenate([ref[c, start : start + size, :] for c in range(ref.shape[0])], axis=1)


def one_hot(row, count):
    nodes = lax.broadcasted_iota(I32, (count, row.shape[1]), 0)
    return jnp.where(nodes == row, 1.0, 0.0).astype(BF16)


def code_table(digits, table, core, rows_used):
    width = table.shape[1]
    value = table[...] + 1
    digits[...] = jnp.zeros_like(digits)
    digits[0:5, 0:width] = (value >> 4).astype(F32)
    digits[8:13, 0:width] = (value & 15).astype(F32)
    row = lax.broadcasted_iota(I32, (TILE, 16), 0)
    col = lax.broadcasted_iota(I32, (TILE, 16), 1)
    near = row & 15
    base = jnp.where((row >> 4) == core, 3, 0)
    wanted = (near & 1) * 8 + base + ((near >> 1) & 1)
    total = None
    for k in range(width // LANES):
        pick = jnp.where((col == wanted) & ((near >> 2) == k + rows_used), 1.0, 0.0).astype(BF16)
        part = dot(pick, digits[:, k * LANES : (k + 1) * LANES].astype(BF16))
        total = part if total is None else total + part
    return total


def decode(tile, offset, second):
    row = lax.broadcasted_iota(I32, (8, TILE), 0)
    col = lax.broadcasted_iota(I32, (8, TILE), 1)
    place = offset + (row & 3) * 4 + second * 2
    weight = jnp.where(col == place, 16.0, jnp.where(col == place + 1, 1.0, 0.0))
    return dot(weight.astype(BF16), tile).astype(I32) - 1


def pre_kernel(
    grid_state, big, w_es, w_ed, w_dd, enc_src, enc_dst, dec_src, dec_dst, proc_src, proc_dst,
    payload, enc_recv, dec_recv, latent, digits,
):
    core = lax.axis_index("core")
    channels = grid_state.shape[1]
    nodes = grid_state.shape[0]
    grid_latent = silu(dot(grid_state[...], wide(big, 0, channels))).astype(BF16)
    latent[...] = grid_latent
    grid_normed = rms(grid_latent).astype(BF16)
    payload[0:nodes, :] = dot(grid_normed, w_es[...]).astype(BF16)
    dec_recv[...] = dot(grid_normed, w_dd[...]).astype(BF16)
    mesh_count = enc_recv.shape[0]
    mesh_normed = rms(wide(big, big.shape[1] - mesh_count, mesh_count)).astype(BF16)
    enc_recv[...] = dot(mesh_normed, w_ed[...]).astype(BF16)
    for t, table in enumerate((enc_src, enc_dst, dec_src, dec_dst)):
        start = nodes + t * TILE
        payload[start : start + TILE, :] = code_table(digits, table, core, 0).astype(BF16)
    start = nodes + 4 * TILE
    both = code_table(digits, proc_src, core, 0) + code_table(digits, proc_dst, core, 1)
    payload[start : start + TILE, :] = both.astype(BF16)


def add_edges(total, send_t, recv_t, src, dst, send_count, recv_count):
    to = one_hot(dst, recv_count)
    message = silu(dot(send_t, one_hot(src, send_count)) + dot(recv_t, to)).astype(BF16)
    part = dot_last(message, to)
    return part if total is None else total + part


def flat(rows, start, count):
    return jnp.concatenate([rows[start + k : start + k + 1, :] for k in range(count)], axis=1)


def places(core):
    sib = 1 - core
    return (
        ("two", 0, core * 16, 1),
        ("two", 1, 16 - core * 16, 0),
        ("pair", sib, 0, sib),
        ("far", core, 16, core),
    )


def transposed(values):
    return values.astype(F32).T.astype(BF16)


def enc_kernel(
    pair, two, recv, enc_src, enc_dst,
    agg, proc_tab, dec_tab,
):
    core = lax.axis_index("core")
    sib = 1 - core
    recv_count = recv.shape[0]
    send_count = pair.shape[1] - TABLES * TILE
    recv_t = transposed(recv[...])
    total = add_edges(
        None, transposed(pair[core, 0:send_count, :]), recv_t, enc_src[2:3, :], enc_dst[2:3, :],
        send_count, recv_count,
    )
    for v, (kind, place, offset, second) in enumerate(places(core)):
        if kind == "two":
            block = two.at[core, place]
        elif kind == "pair":
            block = pair.at[sib]
        else:
            block = two.at[sib, core]
        lists = [
            decode(block[send_count + t * TILE : send_count + (t + 1) * TILE, :], offset, second)
            for t in range(TABLES)
        ]
        total = add_edges(
            total, transposed(block[0:send_count, :]), recv_t, flat(lists[0], 0, 4), flat(lists[1], 0, 4),
            send_count, recv_count,
        )
        dec_tab[0, v] = lists[2]
        dec_tab[1, v] = lists[3]
        proc_tab[v] = lists[4]
    agg[...] = total.T.astype(BF16)


def node_kernel(has_recv, agg4, state, weights, w_send, *rest):
    if has_recv:
        w_recv, new_state, send, recv = rest
    else:
        (send,) = rest
    count = agg4.shape[1]
    agg = wide(agg4, 0, count)
    if len(state.shape) == 3:
        before = wide(state, state.shape[1] - count, count).astype(F32)
    else:
        before = state[...]
    after = before + dot(rms(agg).astype(BF16), wide(weights, 0, weights.shape[1]))
    normed = rms(after.astype(BF16)).astype(BF16)
    send[...] = dot(normed, w_send[...]).astype(BF16)
    if has_recv:
        new_state[...] = after
        recv[...] = dot(normed, w_recv[...]).astype(BF16)


def proc_kernel(pair, two, recv, local_src, local_dst, proc_src, proc_dst, tab, agg):
    core = lax.axis_index("core")
    sib = 1 - core
    count = recv.shape[0]
    recv_t = transposed(recv[...])
    own_src = jnp.concatenate([local_src[...], proc_src[2:3, :]], axis=1)
    own_dst = jnp.concatenate([local_dst[...], proc_dst[2:3, :]], axis=1)
    total = add_edges(None, transposed(pair[core]), recv_t, own_src, own_dst, count, count)
    for v, block in enumerate((two.at[core, 0], two.at[core, 1], pair.at[sib], two.at[sib, core])):
        lists = tab[v]
        total = add_edges(
            total, transposed(block[...]), recv_t, lists[0:1, :], lists[1:2, :], count, count
        )
    agg[...] = total.T.astype(BF16)


def dec_kernel(pair, two, recv, dec_src, dec_dst, tab, agg):
    core = lax.axis_index("core")
    sib = 1 - core
    recv_count = recv.shape[0]
    send_count = pair.shape[1]
    recv_t = transposed(recv[...])
    total = add_edges(
        None, transposed(pair[core]), recv_t, dec_src[2:3, :], dec_dst[2:3, :], send_count, recv_count
    )
    for v, block in enumerate((two.at[core, 0], two.at[core, 1], pair.at[sib], two.at[sib, core])):
        total = add_edges(
            total, transposed(block[...]), recv_t, flat(tab[0, v], 0, 4), flat(tab[1, v], 0, 4),
            send_count, recv_count,
        )
    agg[...] = total.T.astype(BF16)


def out_kernel(agg4, latent, weights, out):
    combined = wide(agg4, 0, agg4.shape[1]).astype(F32) + latent[...].astype(F32)
    normed = rms(combined).astype(BF16)
    rows = weights.shape[1]
    parts = weights.shape[0]
    low = jnp.concatenate([weights[c, rows - 256 : rows - 128, :] for c in range(parts)], axis=0)
    high = jnp.concatenate([weights[c, rows - 128 : rows, :] for c in range(parts)], axis=0)
    columns = out.shape[1]
    out[:, 0:LANES] = dot(normed, low).astype(BF16)
    out[:, LANES:columns] = dot(normed, high)[:, 0 : columns - LANES].astype(BF16)


def call(kernel, out_shapes, *args, scratch=()):
    return pl.pallas_call(
        kernel,
        out_shape=out_shapes,
        in_specs=[pl.BlockSpec(memory_space=pltpu.VMEM)] * len(args),
        out_specs=jax.tree.map(lambda _: pl.BlockSpec(memory_space=pltpu.VMEM), out_shapes),
        scratch_shapes=scratch,
        compiler_params=pltpu.CompilerParams(vmem_limit_bytes=40 * 1024 * 1024),
    )(*args)


def shape(dims, kind=BF16):
    return jax.ShapeDtypeStruct(dims, kind)


def chan_gather(block):
    count = lax.axis_size("chan")
    copies = jnp.broadcast_to(block[None], (count,) + block.shape)
    return lax.all_to_all(copies, "chan", 0, 0, tiled=True)


def around(block):
    pair = lax.all_gather(block, "core")
    parts = lax.axis_size(("pair", "core"))
    swap = [(s, (s + 1) % parts if s % 2 else (s - 1) % parts) for s in range(parts)]
    got = lax.ppermute(pair, ("pair", "core"), swap)
    return pair, lax.all_gather(got, "core")


def on_device(
    grid_state, mesh_latent, w_in, w_enc_src, w_enc_dst, w_enc_out, w_proc, w_dec_src, w_dec_dst, w_out,
    enc_src, enc_dst, local_src, local_dst, proc_src, proc_dst, dec_src, dec_dst,
):
    grid_count, channels = grid_state.shape
    mesh_count, width = mesh_latent.shape
    chans = lax.axis_size("chan")
    latent_width = width * chans

    w_out_pad = jnp.pad(w_out, ((0, 0), (0, 2 * LANES - channels)))
    late = jnp.concatenate(
        [w_enc_out, w_proc[0, 2], w_proc[1, 2], w_out_pad[:, :LANES], w_out_pad[:, LANES:]], axis=0
    )
    late = lax.all_gather(late, "chan")
    updates = [late[:, i * latent_width : (i + 1) * latent_width] for i in range(3)]

    early = jnp.concatenate([jnp.pad(w_in, ((0, 2 * LANES - channels), (0, 0))), mesh_latent], axis=0)
    big = chan_gather(early)

    payload, recv, dec_recv, grid_latent = call(
        pre_kernel,
        (
            shape((grid_count + TABLES * TILE, width)),
            shape((mesh_count, width)),
            shape((grid_count, width)),
            shape((grid_count, latent_width)),
        ),
        grid_state, big, w_enc_src, w_enc_dst, w_dec_dst,
        enc_src, enc_dst, dec_src, dec_dst, proc_src, proc_dst,
        scratch=[pltpu.VMEM((16, enc_src.shape[1]), F32)],
    )
    pair, two = around(payload)
    agg, proc_tab, dec_tab = call(
        enc_kernel,
        (shape((mesh_count, width)), shape((4, 8, LANES), I32), shape((2, 4, 8, LANES), I32)),
        pair, two, recv, enc_src, enc_dst,
    )
    state = big
    for layer in range(w_proc.shape[0]):
        state, send, recv = call(
            lambda *refs: node_kernel(True, *refs),
            (shape((mesh_count, latent_width), F32), shape((mesh_count, width)), shape((mesh_count, width))),
            chan_gather(agg), state, updates[layer], w_proc[layer, 0], w_proc[layer, 1],
        )
        pair, two = around(send)
        agg = call(
            proc_kernel, shape((mesh_count, width)),
            pair, two, recv, local_src, local_dst, proc_src, proc_dst, proc_tab,
        )
    send = call(
        lambda *refs: node_kernel(False, *refs[:4], refs[4]), shape((mesh_count, width)),
        chan_gather(agg), state, updates[2], w_dec_src,
    )
    pair, two = around(send)
    agg = call(
        dec_kernel, shape((grid_count, width)), pair, two, dec_recv, dec_src, dec_dst, dec_tab
    )
    return call(out_kernel, shape((grid_count, channels)), chan_gather(agg), grid_latent, late)


def solution(mesh):
    bands, chans = mesh.devices.shape
    split = Mesh(mesh.devices.reshape(bands // 2, 2, chans), ("pair", "core", "chan"))
    band = ("pair", "core")
    placed = (
        P(band, None),
        P(band, "chan"),
        P(None, "chan"),
        P(None, "chan"),
        P(None, "chan"),
        P(None, "chan"),
        P(None, None, None, "chan"),
        P(None, "chan"),
        P(None, "chan"),
        P("chan", None),
    ) + (P(band, None),) * 8
    return jax.shard_map(
        on_device, mesh=split, in_specs=placed, out_specs=P(band, None), check_vma=False
    )
```

```python
import functools

import jax
import jax.numpy as jnp
from jax import lax
from jax.experimental import pallas as pl
from jax.experimental.pallas import tpu as pltpu
from jax.sharding import PartitionSpec as P

EPS = 1e-05
F32 = jnp.float32
BF16 = jnp.bfloat16
I32 = jnp.int32
LANES = 128
TILE = 32
TABLES = 5


def rms(values):
    values = values.astype(F32)
    return values * lax.rsqrt(jnp.mean(values * values, axis=-1, keepdims=True) + EPS)


def silu(values):
    return 0.5 * values * (1.0 + jnp.tanh(0.5 * values))


def dot(a, b):
    return lax.dot_general(a, b, (((1,), (0,)), ((), ())), preferred_element_type=F32)


def dot_first(a, b):
    return lax.dot_general(a, b, (((0,), (0,)), ((), ())), preferred_element_type=F32)


def dot_last(a, b):
    return lax.dot_general(a, b, (((1,), (1,)), ((), ())), preferred_element_type=F32)


def wide(ref, start, size):
    return jnp.concatenate([ref[c, start : start + size, :] for c in range(ref.shape[0])], axis=1)


def core_index():
    return lax.axis_index("band") & 1


def one_hot(row, count):
    nodes = lax.broadcasted_iota(I32, (count, row.shape[1]), 0)
    return jnp.where(nodes == row, 1.0, 0.0).astype(BF16)


def code_table(digits, table, core, rows_used):
    width = table.shape[1]
    value = table[...] + 1
    digits[...] = jnp.zeros_like(digits)
    digits[0:5, 0:width] = (value >> 4).astype(F32)
    digits[8:13, 0:width] = (value & 15).astype(F32)
    row = lax.broadcasted_iota(I32, (TILE, 16), 0)
    col = lax.broadcasted_iota(I32, (TILE, 16), 1)
    near = row & 15
    base = jnp.where((row >> 4) == core, 3, 0)
    wanted = (near & 1) * 8 + base + ((near >> 1) & 1)
    total = None
    for k in range(width // LANES):
        pick = jnp.where((col == wanted) & ((near >> 2) == k + rows_used), 1.0, 0.0).astype(BF16)
        part = dot(pick, digits[:, k * LANES : (k + 1) * LANES].astype(BF16))
        total = part if total is None else total + part
    return total


def decode(tile, offset, second):
    row = lax.broadcasted_iota(I32, (8, TILE), 0)
    col = lax.broadcasted_iota(I32, (8, TILE), 1)
    place = offset + (row & 3) * 4 + second * 2
    weight = jnp.where(col == place, 16.0, jnp.where(col == place + 1, 1.0, 0.0))
    return dot(weight.astype(BF16), tile).astype(I32) - 1


def pre_kernel(
    grid_state, big, w_es, w_ed, w_dd, enc_src, enc_dst, dec_src, dec_dst, proc_src, proc_dst,
    payload, enc_recv, dec_recv, latent, digits,
):
    core = core_index()
    channels, nodes = grid_state.shape
    grid_latent = silu(dot_first(grid_state[...], wide(big, 0, channels))).astype(BF16)
    latent[...] = grid_latent
    grid_normed = rms(grid_latent).astype(BF16)
    payload[0:nodes, :] = dot(grid_normed, w_es[...]).astype(BF16)
    dec_recv[...] = dot(grid_normed, w_dd[...]).astype(BF16)
    mesh_count = enc_recv.shape[0]
    mesh_normed = rms(wide(big, big.shape[1] - mesh_count, mesh_count)).astype(BF16)
    enc_recv[...] = dot(mesh_normed, w_ed[...]).astype(BF16)
    for t, table in enumerate((enc_src, enc_dst, dec_src, dec_dst)):
        start = nodes + t * TILE
        payload[start : start + TILE, :] = code_table(digits, table, core, 0).astype(BF16)
    start = nodes + 4 * TILE
    both = code_table(digits, proc_src, core, 0) + code_table(digits, proc_dst, core, 1)
    payload[start : start + TILE, :] = both.astype(BF16)


def add_edges(total, send_t, recv_t, src, dst, send_count, recv_count):
    to = one_hot(dst, recv_count)
    message = silu(dot(send_t, one_hot(src, send_count)) + dot(recv_t, to)).astype(BF16)
    part = dot_last(message, to)
    return part if total is None else total + part


def flat(rows, start, count):
    return jnp.concatenate([rows[start + k : start + k + 1, :] for k in range(count)], axis=1)


def places(core):
    sib = 1 - core
    return (
        ("two", 0, core * 16, 1),
        ("two", 1, 16 - core * 16, 0),
        ("pair", sib, 0, sib),
        ("far", core, 16, core),
    )


def transposed(values):
    return values.astype(F32).T.astype(BF16)


def enc_kernel(
    pair, two, far, recv, enc_src, enc_dst,
    agg, proc_tab, dec_tab,
):
    core = core_index()
    sib = 1 - core
    recv_count = recv.shape[0]
    send_count = pair.shape[1] - TABLES * TILE
    recv_t = transposed(recv[...])
    total = add_edges(
        None, transposed(pair[core, 0:send_count, :]), recv_t, enc_src[2:3, :], enc_dst[2:3, :],
        send_count, recv_count,
    )
    for v, (kind, place, offset, second) in enumerate(places(core)):
        if kind == "two":
            block = two.at[core, place]
        elif kind == "pair":
            block = pair.at[sib]
        else:
            block = far.at[sib]
        lists = [
            decode(block[send_count + t * TILE : send_count + (t + 1) * TILE, :], offset, second)
            for t in range(TABLES)
        ]
        total = add_edges(
            total, transposed(block[0:send_count, :]), recv_t, flat(lists[0], 0, 4), flat(lists[1], 0, 4),
            send_count, recv_count,
        )
        dec_tab[0, v] = lists[2]
        dec_tab[1, v] = lists[3]
        proc_tab[v] = lists[4]
    agg[...] = jnp.broadcast_to(total.T.astype(BF16)[None], agg.shape)


def rows_of(late, start, size):
    half = late.shape[2]
    parts = []
    while size > 0:
        k, low = start // half, start % half
        take = min(size, half - low)
        parts.append(
            jnp.concatenate([late[k, c, low : low + take, :] for c in range(late.shape[1])], axis=1)
        )
        start, size = start + take, size - take
    return parts[0] if len(parts) == 1 else jnp.concatenate(parts, axis=0)


def early_kernel(w_in, mesh_latent, out):
    channels = w_in.shape[0]
    start = out.shape[1] - mesh_latent.shape[0]
    for c in range(out.shape[0]):
        out[c, 0:channels, :] = w_in[...]
        out[c, start:, :] = mesh_latent[...]


def late_kernel(w_enc_out, w_proc, w_out, out):
    core = core_index()
    half = out.shape[1]
    depth = w_enc_out.shape[0]
    for k in range(2):

        @pl.when(core == k)
        def _():
            for i in range(4):
                block = (w_enc_out, w_proc.at[0, 2], w_proc.at[1, 2], w_out)[i]
                low = max(i * depth, k * half)
                high = min(i * depth + block.shape[0], (k + 1) * half)
                if low < high:
                    rows = block[low - i * depth : high - i * depth, :]
                    for c in range(out.shape[0]):
                        out[c, low - k * half : high - k * half, :] = rows


def node_kernel(index, has_recv, agg4, state, weights, w_send, *rest):
    if has_recv:
        w_recv, new_state, send, recv = rest
    else:
        (send,) = rest
    count = agg4.shape[1]
    agg = wide(agg4, 0, count)
    if len(state.shape) == 3:
        before = wide(state, state.shape[1] - count, count).astype(F32)
    else:
        before = state[...]
    after = before + dot(rms(agg).astype(BF16), rows_of(weights, index * agg.shape[1], agg.shape[1]))
    normed = rms(after.astype(BF16)).astype(BF16)
    send[...] = dot(normed, w_send[...]).astype(BF16)
    if has_recv:
        new_state[...] = after
        recv[...] = dot(normed, w_recv[...]).astype(BF16)


def proc_kernel(pair, two, far, recv, local_src, local_dst, proc_src, proc_dst, tab, agg):
    core = core_index()
    sib = 1 - core
    count = recv.shape[0]
    recv_t = transposed(recv[...])
    own_src = jnp.concatenate([local_src[...], proc_src[2:3, :]], axis=1)
    own_dst = jnp.concatenate([local_dst[...], proc_dst[2:3, :]], axis=1)
    total = add_edges(None, transposed(pair[core]), recv_t, own_src, own_dst, count, count)
    for v, block in enumerate((two.at[core, 0], two.at[core, 1], pair.at[sib], far.at[sib])):
        lists = tab[v]
        total = add_edges(
            total, transposed(block[...]), recv_t, lists[0:1, :], lists[1:2, :], count, count
        )
    agg[...] = jnp.broadcast_to(total.T.astype(BF16)[None], agg.shape)


def dec_kernel(pair, two, far, recv, dec_src, dec_dst, tab, agg):
    core = core_index()
    sib = 1 - core
    recv_count = recv.shape[0]
    send_count = pair.shape[1]
    recv_t = transposed(recv[...])
    total = add_edges(
        None, transposed(pair[core]), recv_t, dec_src[2:3, :], dec_dst[2:3, :], send_count, recv_count
    )
    for v, block in enumerate((two.at[core, 0], two.at[core, 1], pair.at[sib], far.at[sib])):
        total = add_edges(
            total, transposed(block[...]), recv_t, flat(tab[0, v], 0, 4), flat(tab[1, v], 0, 4),
            send_count, recv_count,
        )
    agg[...] = jnp.broadcast_to(total.T.astype(BF16)[None], agg.shape)


def out_kernel(agg4, latent, weights, out):
    combined = wide(agg4, 0, agg4.shape[1]).astype(F32) + latent[...].astype(F32)
    normed = rms(combined).astype(BF16)
    out[...] = dot_last(rows_of(weights, 3 * normed.shape[1], out.shape[0]), normed).astype(BF16)


def call(kernel, out_shapes, *args, scratch=()):
    return pl.pallas_call(
        kernel,
        out_shape=out_shapes,
        in_specs=[pl.BlockSpec(memory_space=pltpu.VMEM)] * len(args),
        out_specs=jax.tree.map(lambda _: pl.BlockSpec(memory_space=pltpu.VMEM), out_shapes),
        scratch_shapes=scratch,
        compiler_params=pltpu.CompilerParams(vmem_limit_bytes=40 * 1024 * 1024),
    )(*args)


def shape(dims, kind=BF16):
    return jax.ShapeDtypeStruct(dims, kind)


def exchange(copies):
    return lax.all_to_all(copies, "chan", 0, 0, tiled=True)


def core_gather(block):
    parts = lax.axis_size("band")
    return lax.all_gather(block, "band", axis_index_groups=[[s, s + 1] for s in range(0, parts, 2)])


def around(block):
    parts = lax.axis_size("band")
    pair = core_gather(block)
    sides = [[s, (s + 1) % parts] for s in range(1, parts, 2)]
    two = lax.all_gather(pair, "band", axis_index_groups=sides)
    near = jnp.where(core_index() == 0, two[0, 1], two[1, 0])
    return pair, two, core_gather(near)


def on_device(
    grid_state, mesh_latent, w_in, w_enc_src, w_enc_dst, w_enc_out, w_proc, w_dec_src, w_dec_dst, w_out,
    enc_src, enc_dst, local_src, local_dst, proc_src, proc_dst, dec_src, dec_dst,
):
    grid_count, channels = grid_state.shape
    mesh_count, width = mesh_latent.shape
    chans = lax.axis_size("chan")
    latent_width = width * chans

    channel_rows = -(-channels // LANES) * LANES
    late_rows = 3 * latent_width + channel_rows
    big = exchange(call(
        early_kernel, shape((chans, channel_rows + mesh_count, width)), w_in, mesh_latent
    ))
    late = core_gather(exchange(call(
        late_kernel, shape((chans, late_rows // 2, width)), w_enc_out, w_proc, w_out.T
    )))

    payload, recv, dec_recv, grid_latent = call(
        pre_kernel,
        (
            shape((grid_count + TABLES * TILE, width)),
            shape((mesh_count, width)),
            shape((grid_count, width)),
            shape((grid_count, latent_width)),
        ),
        grid_state.T, big, w_enc_src, w_enc_dst, w_dec_dst,
        enc_src, enc_dst, dec_src, dec_dst, proc_src, proc_dst,
        scratch=[pltpu.VMEM((16, enc_src.shape[1]), F32)],
    )
    pair, two, far = around(payload)
    agg, proc_tab, dec_tab = call(
        enc_kernel,
        (shape((chans, mesh_count, width)), shape((4, 8, LANES), I32), shape((2, 4, 8, LANES), I32)),
        pair, two, far, recv, enc_src, enc_dst,
    )
    state = big
    for layer in range(w_proc.shape[0]):
        state, send, recv = call(
            functools.partial(node_kernel, layer, True),
            (shape((mesh_count, latent_width), F32), shape((mesh_count, width)), shape((mesh_count, width))),
            exchange(agg), state, late, w_proc[layer, 0], w_proc[layer, 1],
        )
        pair, two, far = around(send)
        agg = call(
            proc_kernel, shape((chans, mesh_count, width)),
            pair, two, far, recv, local_src, local_dst, proc_src, proc_dst, proc_tab,
        )
    send = call(
        functools.partial(node_kernel, w_proc.shape[0], False), shape((mesh_count, width)),
        exchange(agg), state, late, w_dec_src,
    )
    pair, two, far = around(send)
    agg = call(
        dec_kernel, shape((chans, grid_count, width)), pair, two, far, dec_recv, dec_src, dec_dst, dec_tab
    )
    return call(out_kernel, shape((channels, grid_count)), exchange(agg), grid_latent, late).T


def solution(mesh):
    placed = (
        P("band", None),
        P("band", "chan"),
        P(None, "chan"),
        P(None, "chan"),
        P(None, "chan"),
        P(None, "chan"),
        P(None, None, None, "chan"),
        P(None, "chan"),
        P(None, "chan"),
        P("chan", None),
    ) + (P("band", None),) * 8
    return jax.shard_map(
        on_device, mesh=mesh, in_specs=placed, out_specs=P("band", None), check_vma=False
    )
```

```python
import functools

import jax
import jax.numpy as jnp
from jax import lax
from jax.experimental import pallas as pl
from jax.experimental.pallas import tpu as pltpu
from jax.sharding import PartitionSpec as P

EPS = 1e-05
F32 = jnp.float32
BF16 = jnp.bfloat16
I32 = jnp.int32
LANES = 128
TILE = 32
TABLES = 5


def rms(values):
    values = values.astype(F32)
    return values * lax.rsqrt(jnp.mean(values * values, axis=-1, keepdims=True) + EPS)


def silu(values):
    return 0.5 * values * (1.0 + jnp.tanh(0.5 * values))


def dot(a, b):
    return lax.dot_general(a, b, (((1,), (0,)), ((), ())), preferred_element_type=F32)


def dot_first(a, b):
    return lax.dot_general(a, b, (((0,), (0,)), ((), ())), preferred_element_type=F32)


def dot_last(a, b):
    return lax.dot_general(a, b, (((1,), (1,)), ((), ())), preferred_element_type=F32)


def wide(ref, start, size):
    return jnp.concatenate([ref[c, start : start + size, :] for c in range(ref.shape[0])], axis=1)


def core_index():
    return lax.axis_index("band") & 1


def one_hot(row, count):
    nodes = lax.broadcasted_iota(I32, (count, row.shape[1]), 0)
    return jnp.where(nodes == row, 1.0, 0.0).astype(BF16)


def code_table(digits, table, core, rows_used):
    width = table.shape[1]
    value = table[...] + 1
    digits[...] = jnp.zeros_like(digits)
    digits[0:5, 0:width] = (value >> 4).astype(F32)
    digits[8:13, 0:width] = (value & 15).astype(F32)
    row = lax.broadcasted_iota(I32, (TILE, 16), 0)
    col = lax.broadcasted_iota(I32, (TILE, 16), 1)
    near = row & 15
    base = jnp.where((row >> 4) == core, 3, 0)
    wanted = (near & 1) * 8 + base + ((near >> 1) & 1)
    total = None
    for k in range(width // LANES):
        pick = jnp.where((col == wanted) & ((near >> 2) == k + rows_used), 1.0, 0.0).astype(BF16)
        part = dot(pick, digits[:, k * LANES : (k + 1) * LANES].astype(BF16))
        total = part if total is None else total + part
    return total


def decode(tile, offset, second):
    row = lax.broadcasted_iota(I32, (8, TILE), 0)
    col = lax.broadcasted_iota(I32, (8, TILE), 1)
    place = offset + (row & 3) * 4 + second * 2
    weight = jnp.where(col == place, 16.0, jnp.where(col == place + 1, 1.0, 0.0))
    return dot(weight.astype(BF16), tile).astype(I32) - 1


def pre_kernel(
    grid_state, big, w_es, w_ed, w_dd, enc_src, enc_dst, dec_src, dec_dst, proc_src, proc_dst,
    payload, enc_recv, dec_recv, latent, digits,
):
    core = core_index()
    channels, nodes = grid_state.shape
    grid_latent = silu(dot_first(grid_state[...], wide(big, 0, channels))).astype(BF16)
    latent[...] = grid_latent
    grid_normed = rms(grid_latent).astype(BF16)
    payload[0:nodes, :] = dot(grid_normed, w_es[...]).astype(BF16)
    dec_recv[...] = dot(grid_normed, w_dd[...]).astype(BF16)
    mesh_count = enc_recv.shape[0]
    mesh_normed = rms(wide(big, big.shape[1] - mesh_count, mesh_count)).astype(BF16)
    enc_recv[...] = dot(mesh_normed, w_ed[...]).astype(BF16)
    for t, table in enumerate((enc_src, enc_dst, dec_src, dec_dst)):
        start = nodes + t * TILE
        payload[start : start + TILE, :] = code_table(digits, table, core, 0).astype(BF16)
    start = nodes + 4 * TILE
    both = code_table(digits, proc_src, core, 0) + code_table(digits, proc_dst, core, 1)
    payload[start : start + TILE, :] = both.astype(BF16)


def add_edges(total, send_t, recv_t, src, dst, send_count, recv_count):
    to = one_hot(dst, recv_count)
    message = silu(dot(send_t, one_hot(src, send_count)) + dot(recv_t, to)).astype(BF16)
    part = dot_last(message, to)
    return part if total is None else total + part


def flat(rows, start, count):
    return jnp.concatenate([rows[start + k : start + k + 1, :] for k in range(count)], axis=1)


def places(core):
    sib = 1 - core
    return (
        ("two", 0, core * 16, 1),
        ("two", 1, 16 - core * 16, 0),
        ("pair", sib, 0, sib),
        ("far", core, 16, core),
    )


def transposed(values):
    return values.astype(F32).T.astype(BF16)


def enc_kernel(
    pair, two, far, recv, enc_src, enc_dst,
    agg, proc_tab, dec_tab,
):
    core = core_index()
    sib = 1 - core
    recv_count = recv.shape[0]
    send_count = pair.shape[1] - TABLES * TILE
    recv_t = transposed(recv[...])
    total = add_edges(
        None, transposed(pair[core, 0:send_count, :]), recv_t, enc_src[2:3, :], enc_dst[2:3, :],
        send_count, recv_count,
    )
    for v, (kind, place, offset, second) in enumerate(places(core)):
        if kind == "two":
            block = two.at[core, place]
        elif kind == "pair":
            block = pair.at[sib]
        else:
            block = far.at[sib]
        lists = [
            decode(block[send_count + t * TILE : send_count + (t + 1) * TILE, :], offset, second)
            for t in range(TABLES)
        ]
        total = add_edges(
            total, transposed(block[0:send_count, :]), recv_t, flat(lists[0], 0, 4), flat(lists[1], 0, 4),
            send_count, recv_count,
        )
        dec_tab[0, v] = lists[2]
        dec_tab[1, v] = lists[3]
        proc_tab[v] = lists[4]
    agg[...] = jnp.broadcast_to(total.T.astype(BF16)[None], agg.shape)


def rows_of(mine, other, start, size):
    core = core_index()
    half = mine.shape[1]
    parts = []
    while size > 0:
        k, low = start // half, start % half
        take = min(size, half - low)
        parts.append(
            jnp.where(core == k, wide(mine, low, take), wide(other, low, take))
        )
        start, size = start + take, size - take
    return parts[0] if len(parts) == 1 else jnp.concatenate(parts, axis=0)


def early_kernel(w_in, mesh_latent, out):
    channels = w_in.shape[0]
    start = out.shape[1] - mesh_latent.shape[0]
    for c in range(out.shape[0]):
        out[c, 0:channels, :] = w_in[...]
        out[c, start:, :] = mesh_latent[...]


def late_kernel(w_enc_out, w_proc, w_out, out):
    core = core_index()
    half = out.shape[1]
    depth = w_enc_out.shape[0]
    for k in range(2):

        @pl.when(core == k)
        def _():
            for i in range(4):
                block = (w_enc_out, w_proc.at[0, 2], w_proc.at[1, 2], w_out)[i]
                low = max(i * depth, k * half)
                high = min(i * depth + block.shape[0], (k + 1) * half)
                if low < high:
                    rows = block[low - i * depth : high - i * depth, :]
                    for c in range(out.shape[0]):
                        out[c, low - k * half : high - k * half, :] = rows


def node_kernel(index, has_recv, agg4, state, mine, other, w_send, *rest):
    if has_recv:
        w_recv, new_state, send, recv = rest
    else:
        (send,) = rest
    count = agg4.shape[1]
    agg = wide(agg4, 0, count)
    if len(state.shape) == 3:
        before = wide(state, state.shape[1] - count, count).astype(F32)
    else:
        before = state[...]
    after = before + dot(rms(agg).astype(BF16), rows_of(mine, other, index * agg.shape[1], agg.shape[1]))
    normed = rms(after.astype(BF16)).astype(BF16)
    send[...] = dot(normed, w_send[...]).astype(BF16)
    if has_recv:
        new_state[...] = after
        recv[...] = dot(normed, w_recv[...]).astype(BF16)


def proc_kernel(pair, two, far, recv, local_src, local_dst, proc_src, proc_dst, tab, agg):
    core = core_index()
    sib = 1 - core
    count = recv.shape[0]
    recv_t = transposed(recv[...])
    own_src = jnp.concatenate([local_src[...], proc_src[2:3, :]], axis=1)
    own_dst = jnp.concatenate([local_dst[...], proc_dst[2:3, :]], axis=1)
    total = add_edges(None, transposed(pair[core]), recv_t, own_src, own_dst, count, count)
    for v, block in enumerate((two.at[core, 0], two.at[core, 1], pair.at[sib], far.at[sib])):
        lists = tab[v]
        total = add_edges(
            total, transposed(block[...]), recv_t, lists[0:1, :], lists[1:2, :], count, count
        )
    agg[...] = jnp.broadcast_to(total.T.astype(BF16)[None], agg.shape)


def dec_kernel(pair, two, far, recv, dec_src, dec_dst, tab, agg):
    core = core_index()
    sib = 1 - core
    recv_count = recv.shape[0]
    send_count = pair.shape[1]
    recv_t = transposed(recv[...])
    total = add_edges(
        None, transposed(pair[core]), recv_t, dec_src[2:3, :], dec_dst[2:3, :], send_count, recv_count
    )
    for v, block in enumerate((two.at[core, 0], two.at[core, 1], pair.at[sib], far.at[sib])):
        total = add_edges(
            total, transposed(block[...]), recv_t, flat(tab[0, v], 0, 4), flat(tab[1, v], 0, 4),
            send_count, recv_count,
        )
    agg[...] = jnp.broadcast_to(total.T.astype(BF16)[None], agg.shape)


def out_kernel(agg4, latent, mine, other, out):
    combined = wide(agg4, 0, agg4.shape[1]).astype(F32) + latent[...].astype(F32)
    normed = rms(combined).astype(BF16)
    out[...] = dot_last(rows_of(mine, other, 3 * normed.shape[1], out.shape[0]), normed).astype(BF16)


def call(kernel, out_shapes, *args, scratch=()):
    return pl.pallas_call(
        kernel,
        out_shape=out_shapes,
        in_specs=[pl.BlockSpec(memory_space=pltpu.VMEM)] * len(args),
        out_specs=jax.tree.map(lambda _: pl.BlockSpec(memory_space=pltpu.VMEM), out_shapes),
        scratch_shapes=scratch,
        compiler_params=pltpu.CompilerParams(vmem_limit_bytes=40 * 1024 * 1024),
    )(*args)


def shape(dims, kind=BF16):
    return jax.ShapeDtypeStruct(dims, kind)


def exchange(copies):
    return lax.all_to_all(copies, "chan", 0, 0, tiled=True)


def core_gather(block):
    parts = lax.axis_size("band")
    return lax.all_gather(block, "band", axis_index_groups=[[s, s + 1] for s in range(0, parts, 2)])


def around(block):
    parts = lax.axis_size("band")
    pair = core_gather(block)
    sides = [[s, (s + 1) % parts] for s in range(1, parts, 2)]
    two = lax.all_gather(pair, "band", axis_index_groups=sides)
    near = jnp.where(core_index() == 0, two[0, 1], two[1, 0])
    return pair, two, core_gather(near)


def on_device(
    grid_state, mesh_latent, w_in, w_enc_src, w_enc_dst, w_enc_out, w_proc, w_dec_src, w_dec_dst, w_out,
    enc_src, enc_dst, local_src, local_dst, proc_src, proc_dst, dec_src, dec_dst,
):
    grid_count, channels = grid_state.shape
    mesh_count, width = mesh_latent.shape
    chans = lax.axis_size("chan")
    latent_width = width * chans

    channel_rows = -(-channels // LANES) * LANES
    late_rows = 3 * latent_width + channel_rows
    big = exchange(call(
        early_kernel, shape((chans, channel_rows + mesh_count, width)), w_in, mesh_latent
    ))
    copies = call(
        late_kernel, shape((chans, late_rows // 2, width)), w_enc_out, w_proc, w_out.T
    )
    copies, big = lax.optimization_barrier((copies, big))
    mine = exchange(copies)
    other = lax.ppermute(mine, "band", [(s, s ^ 1) for s in range(lax.axis_size("band"))])

    payload, recv, dec_recv, grid_latent = call(
        pre_kernel,
        (
            shape((grid_count + TABLES * TILE, width)),
            shape((mesh_count, width)),
            shape((grid_count, width)),
            shape((grid_count, latent_width)),
        ),
        grid_state.T, big, w_enc_src, w_enc_dst, w_dec_dst,
        enc_src, enc_dst, dec_src, dec_dst, proc_src, proc_dst,
        scratch=[pltpu.VMEM((16, enc_src.shape[1]), F32)],
    )
    pair, two, far = around(payload)
    agg, proc_tab, dec_tab = call(
        enc_kernel,
        (shape((chans, mesh_count, width)), shape((4, 8, LANES), I32), shape((2, 4, 8, LANES), I32)),
        pair, two, far, recv, enc_src, enc_dst,
    )
    state = big
    for layer in range(w_proc.shape[0]):
        state, send, recv = call(
            functools.partial(node_kernel, layer, True),
            (shape((mesh_count, latent_width), F32), shape((mesh_count, width)), shape((mesh_count, width))),
            exchange(agg), state, mine, other, w_proc[layer, 0], w_proc[layer, 1],
        )
        pair, two, far = around(send)
        agg = call(
            proc_kernel, shape((chans, mesh_count, width)),
            pair, two, far, recv, local_src, local_dst, proc_src, proc_dst, proc_tab,
        )
    send = call(
        functools.partial(node_kernel, w_proc.shape[0], False), shape((mesh_count, width)),
        exchange(agg), state, mine, other, w_dec_src,
    )
    pair, two, far = around(send)
    agg = call(
        dec_kernel, shape((chans, grid_count, width)), pair, two, far, dec_recv, dec_src, dec_dst, dec_tab
    )
    return call(out_kernel, shape((channels, grid_count)), exchange(agg), grid_latent, mine, other).T


def solution(mesh):
    placed = (
        P("band", None),
        P("band", "chan"),
        P(None, "chan"),
        P(None, "chan"),
        P(None, "chan"),
        P(None, "chan"),
        P(None, None, None, "chan"),
        P(None, "chan"),
        P(None, "chan"),
        P("chan", None),
    ) + (P("band", None),) * 8
    return jax.shard_map(
        on_device, mesh=mesh, in_specs=placed, out_specs=P("band", None), check_vma=False
    )
```

```python
import functools

import jax
import jax.numpy as jnp
from jax import lax
from jax.experimental import pallas as pl
from jax.experimental.pallas import tpu as pltpu
from jax.sharding import PartitionSpec as P

EPS = 1e-05
F32 = jnp.float32
BF16 = jnp.bfloat16
I32 = jnp.int32
LANES = 128
CHANS = 4
TILE = 32
TABLES = 5


def rms(values):
    values = values.astype(F32)
    return values * lax.rsqrt(jnp.mean(values * values, axis=-1, keepdims=True) + EPS)


def silu(values):
    return 0.5 * values * (1.0 + jnp.tanh(0.5 * values))


def dot(a, b):
    return lax.dot_general(a, b, (((1,), (0,)), ((), ())), preferred_element_type=F32)


def dot_first(a, b):
    return lax.dot_general(a, b, (((0,), (0,)), ((), ())), preferred_element_type=F32)


def dot_last(a, b):
    return lax.dot_general(a, b, (((1,), (1,)), ((), ())), preferred_element_type=F32)


def wide(ref, start, size):
    return jnp.concatenate([ref[c, start : start + size, :] for c in range(ref.shape[0])], axis=1)


def core_index():
    return lax.axis_index("band") & 1


def one_hot(row, count):
    nodes = lax.broadcasted_iota(I32, (count, row.shape[1]), 0)
    return jnp.where(nodes == row, 1.0, 0.0).astype(BF16)


def code_table(digits, table, core, rows_used):
    width = table.shape[1]
    value = table[...] + 1
    digits[...] = jnp.zeros_like(digits)
    digits[0:5, 0:width] = (value >> 4).astype(F32)
    digits[8:13, 0:width] = (value & 15).astype(F32)
    row = lax.broadcasted_iota(I32, (TILE, 16), 0)
    col = lax.broadcasted_iota(I32, (TILE, 16), 1)
    near = row & 15
    base = jnp.where((row >> 4) == core, 3, 0)
    wanted = (near & 1) * 8 + base + ((near >> 1) & 1)
    total = None
    for k in range(width // LANES):
        pick = jnp.where((col == wanted) & ((near >> 2) == k + rows_used), 1.0, 0.0).astype(BF16)
        part = dot(pick, digits[:, k * LANES : (k + 1) * LANES].astype(BF16))
        total = part if total is None else total + part
    return total


def decode(tile, offset, second):
    row = lax.broadcasted_iota(I32, (8, TILE), 0)
    col = lax.broadcasted_iota(I32, (8, TILE), 1)
    place = offset + (row & 3) * 4 + second * 2
    weight = jnp.where(col == place, 16.0, jnp.where(col == place + 1, 1.0, 0.0))
    return dot(weight.astype(BF16), tile).astype(I32) - 1


def pre_kernel(
    grid_state, big, w_es, w_ed, w_dd, enc_src, enc_dst, dec_src, dec_dst, proc_src, proc_dst,
    payload, enc_recv, dec_recv, latent, digits,
):
    core = core_index()
    channels, nodes = grid_state.shape
    grid_latent = silu(dot_first(grid_state[...], wide(big, 0, channels))).astype(BF16)
    latent[...] = grid_latent
    grid_normed = rms(grid_latent).astype(BF16)
    payload[0:nodes, :] = dot(grid_normed, w_es[...]).astype(BF16)
    dec_recv[...] = dot(grid_normed, w_dd[...]).astype(BF16)
    mesh_count = enc_recv.shape[0]
    mesh_normed = rms(wide(big, big.shape[1] - mesh_count, mesh_count)).astype(BF16)
    enc_recv[...] = dot(mesh_normed, w_ed[...]).astype(BF16)
    for t, table in enumerate((enc_src, enc_dst, dec_src, dec_dst)):
        start = nodes + t * TILE
        payload[start : start + TILE, :] = code_table(digits, table, core, 0).astype(BF16)
    start = nodes + 4 * TILE
    both = code_table(digits, proc_src, core, 0) + code_table(digits, proc_dst, core, 1)
    payload[start : start + TILE, :] = both.astype(BF16)


def add_edges(total, send_t, recv_t, src, dst, send_count, recv_count):
    to = one_hot(dst, recv_count)
    message = silu(dot(send_t, one_hot(src, send_count)) + dot(recv_t, to)).astype(BF16)
    part = dot_last(message, to)
    return part if total is None else total + part


def flat(rows, start, count):
    return jnp.concatenate([rows[start + k : start + k + 1, :] for k in range(count)], axis=1)


def places(core):
    sib = 1 - core
    return (
        ("two", 0, core * 16, 1),
        ("two", 1, 16 - core * 16, 0),
        ("pair", sib, 0, sib),
        ("far", core, 16, core),
    )


def transposed(values):
    return values.astype(F32).T.astype(BF16)


def enc_kernel(
    pair, two, far, recv, enc_src, enc_dst,
    agg, proc_tab, dec_tab,
):
    core = core_index()
    sib = 1 - core
    recv_count = recv.shape[0]
    send_count = pair.shape[1] - TABLES * TILE
    recv_t = transposed(recv[...])
    total = add_edges(
        None, transposed(pair[core, 0:send_count, :]), recv_t, enc_src[2:3, :], enc_dst[2:3, :],
        send_count, recv_count,
    )
    for v, (kind, place, offset, second) in enumerate(places(core)):
        if kind == "two":
            block = two.at[core, place]
        elif kind == "pair":
            block = pair.at[sib]
        else:
            block = far.at[sib]
        lists = [
            decode(block[send_count + t * TILE : send_count + (t + 1) * TILE, :], offset, second)
            for t in range(TABLES)
        ]
        total = add_edges(
            total, transposed(block[0:send_count, :]), recv_t, flat(lists[0], 0, 4), flat(lists[1], 0, 4),
            send_count, recv_count,
        )
        dec_tab[0, v] = lists[2]
        dec_tab[1, v] = lists[3]
        proc_tab[v] = lists[4]
    agg[...] = jnp.broadcast_to(total.T.astype(BF16)[None], agg.shape)


def source(k):
    return lax.rem(lax.axis_index("chan") + CHANS - k, CHANS)


def arrived(blocks, start, size):
    return jnp.concatenate([block[start : start + size, :] for block in blocks], axis=1)


def columns_at(k):
    return pl.ds(pl.multiple_of(source(k) * LANES, LANES), LANES)


def early_kernel(w_in, mesh_latent, out):
    channels = w_in.shape[0]
    start = out.shape[1] - mesh_latent.shape[0]
    for c in range(out.shape[0]):
        out[c, 0:channels, :] = w_in[...]
        out[c, start:, :] = mesh_latent[...]


def late_kernel(w_enc_out, w_proc, w_out, out):
    depth = w_enc_out.shape[0]
    out[0:depth, :] = w_enc_out[...]
    out[depth : 2 * depth, :] = w_proc[0, 2]
    out[2 * depth : 3 * depth, :] = w_proc[1, 2]
    out[3 * depth : 3 * depth + w_out.shape[0], :] = w_out[...]


def node_kernel(index, has_recv, agg4, state, b0, b1, b2, b3, w_send, *rest):
    if has_recv:
        w_recv, new_state, send, recv = rest
    else:
        (send,) = rest
    count = agg4.shape[1]
    agg = wide(agg4, 0, count)
    if len(state.shape) == 3:
        first = state.shape[1] - count
        before = jnp.concatenate([state[source(k), first:, :] for k in range(CHANS)], axis=1).astype(F32)
    else:
        before = state[...]
    depth = agg.shape[1]
    update = arrived((b0, b1, b2, b3), index * depth, depth)
    after = before + dot(rms(agg).astype(BF16), update)
    normed = rms(after.astype(BF16)).astype(BF16)

    def turned(weight):
        return jnp.concatenate([weight[columns_at(k), :] for k in range(CHANS)], axis=0)

    send[...] = dot(normed, turned(w_send)).astype(BF16)
    if has_recv:
        new_state[...] = after
        recv[...] = dot(normed, turned(w_recv)).astype(BF16)


def proc_kernel(pair, two, far, recv, local_src, local_dst, proc_src, proc_dst, tab, agg):
    core = core_index()
    sib = 1 - core
    count = recv.shape[0]
    recv_t = transposed(recv[...])
    own_src = jnp.concatenate([local_src[...], proc_src[2:3, :]], axis=1)
    own_dst = jnp.concatenate([local_dst[...], proc_dst[2:3, :]], axis=1)
    total = add_edges(None, transposed(pair[core]), recv_t, own_src, own_dst, count, count)
    for v, block in enumerate((two.at[core, 0], two.at[core, 1], pair.at[sib], far.at[sib])):
        lists = tab[v]
        total = add_edges(
            total, transposed(block[...]), recv_t, lists[0:1, :], lists[1:2, :], count, count
        )
    agg[...] = jnp.broadcast_to(total.T.astype(BF16)[None], agg.shape)


def dec_kernel(pair, two, far, recv, dec_src, dec_dst, tab, agg):
    core = core_index()
    sib = 1 - core
    recv_count = recv.shape[0]
    send_count = pair.shape[1]
    recv_t = transposed(recv[...])
    total = add_edges(
        None, transposed(pair[core]), recv_t, dec_src[2:3, :], dec_dst[2:3, :], send_count, recv_count
    )
    for v, block in enumerate((two.at[core, 0], two.at[core, 1], pair.at[sib], far.at[sib])):
        total = add_edges(
            total, transposed(block[...]), recv_t, flat(tab[0, v], 0, 4), flat(tab[1, v], 0, 4),
            send_count, recv_count,
        )
    agg[...] = jnp.broadcast_to(total.T.astype(BF16)[None], agg.shape)


def out_kernel(agg4, latent, b0, b1, b2, b3, out):
    combined = jnp.concatenate(
        [agg4[source(k)].astype(F32) + latent[:, columns_at(k)].astype(F32) for k in range(CHANS)], axis=1
    )
    normed = rms(combined).astype(BF16)
    weights = arrived((b0, b1, b2, b3), 3 * normed.shape[1], out.shape[0])
    out[...] = dot_last(weights, normed).astype(BF16)


def call(kernel, out_shapes, *args, scratch=()):
    return pl.pallas_call(
        kernel,
        out_shape=out_shapes,
        in_specs=[pl.BlockSpec(memory_space=pltpu.VMEM)] * len(args),
        out_specs=jax.tree.map(lambda _: pl.BlockSpec(memory_space=pltpu.VMEM), out_shapes),
        scratch_shapes=scratch,
        compiler_params=pltpu.CompilerParams(vmem_limit_bytes=16 * 1024 * 1024),
    )(*args)


def shape(dims, kind=BF16):
    return jax.ShapeDtypeStruct(dims, kind)


def exchange(copies):
    return lax.all_to_all(copies, "chan", 0, 0, tiled=True)


def core_gather(block):
    parts = lax.axis_size("band")
    return lax.all_gather(block, "band", axis_index_groups=[[s, s + 1] for s in range(0, parts, 2)])


def around(block):
    parts = lax.axis_size("band")
    pair = core_gather(block)
    sides = [[s, (s + 1) % parts] for s in range(1, parts, 2)]
    two = lax.all_gather(pair, "band", axis_index_groups=sides)
    near = jnp.where(core_index() == 0, two[0, 1], two[1, 0])
    return pair, two, core_gather(near)


def on_device(
    grid_state, mesh_latent, w_in, w_enc_src, w_enc_dst, w_enc_out, w_proc, w_dec_src, w_dec_dst, w_out,
    enc_src, enc_dst, local_src, local_dst, proc_src, proc_dst, dec_src, dec_dst,
):
    grid_count, channels = grid_state.shape
    mesh_count, width = mesh_latent.shape
    chans = lax.axis_size("chan")
    latent_width = width * chans

    channel_rows = -(-channels // LANES) * LANES
    late_rows = 3 * latent_width + channel_rows
    big = exchange(call(
        early_kernel, shape((chans, channel_rows + mesh_count, width)), w_in, mesh_latent
    ))
    late = call(late_kernel, shape((late_rows, width)), w_enc_out, w_proc, w_out.T)
    late, big = lax.optimization_barrier((late, big))
    blocks = [late] + [
        lax.ppermute(late, "chan", [(s, (s + k) % chans) for s in range(chans)]) for k in range(1, chans)
    ]

    payload, recv, dec_recv, grid_latent = call(
        pre_kernel,
        (
            shape((grid_count + TABLES * TILE, width)),
            shape((mesh_count, width)),
            shape((grid_count, width)),
            shape((grid_count, latent_width)),
        ),
        grid_state.T, big, w_enc_src, w_enc_dst, w_dec_dst,
        enc_src, enc_dst, dec_src, dec_dst, proc_src, proc_dst,
        scratch=[pltpu.VMEM((16, enc_src.shape[1]), F32)],
    )
    pair, two, far = around(payload)
    agg, proc_tab, dec_tab = call(
        enc_kernel,
        (shape((chans, mesh_count, width)), shape((4, 8, LANES), I32), shape((2, 4, 8, LANES), I32)),
        pair, two, far, recv, enc_src, enc_dst,
    )
    state = big
    for layer in range(w_proc.shape[0]):
        state, send, recv = call(
            functools.partial(node_kernel, layer, True),
            (shape((mesh_count, latent_width), F32), shape((mesh_count, width)), shape((mesh_count, width))),
            exchange(agg), state, *blocks, w_proc[layer, 0], w_proc[layer, 1],
        )
        pair, two, far = around(send)
        agg = call(
            proc_kernel, shape((chans, mesh_count, width)),
            pair, two, far, recv, local_src, local_dst, proc_src, proc_dst, proc_tab,
        )
    send = call(
        functools.partial(node_kernel, w_proc.shape[0], False), shape((mesh_count, width)),
        exchange(agg), state, *blocks, w_dec_src,
    )
    pair, two, far = around(send)
    agg = call(
        dec_kernel, shape((chans, grid_count, width)), pair, two, far, dec_recv, dec_src, dec_dst, dec_tab
    )
    return call(out_kernel, shape((channels, grid_count)), exchange(agg), grid_latent, *blocks).T


def solution(mesh):
    placed = (
        P("band", None),
        P("band", "chan"),
        P(None, "chan"),
        P(None, "chan"),
        P(None, "chan"),
        P(None, "chan"),
        P(None, None, None, "chan"),
        P(None, "chan"),
        P(None, "chan"),
        P("chan", None),
    ) + (P("band", None),) * 8
    return jax.shard_map(
        on_device, mesh=mesh, in_specs=placed, out_specs=P("band", None), check_vma=False
    )
```

```python
import functools

import jax
import jax.numpy as jnp
from jax import lax
from jax.experimental import pallas as pl
from jax.experimental.pallas import tpu as pltpu
from jax.sharding import PartitionSpec as P

EPS = 1e-05
F32 = jnp.float32
BF16 = jnp.bfloat16
I32 = jnp.int32
LANES = 128
CHANS = 4
TILE = 32
TABLES = 5


def rms(values):
    values = values.astype(F32)
    return values * lax.rsqrt(jnp.mean(values * values, axis=-1, keepdims=True) + EPS)


def silu(values):
    return 0.5 * values * (1.0 + jnp.tanh(0.5 * values))


def dot(a, b):
    return lax.dot_general(a, b, (((1,), (0,)), ((), ())), preferred_element_type=F32)


def dot_first(a, b):
    return lax.dot_general(a, b, (((0,), (0,)), ((), ())), preferred_element_type=F32)


def dot_last(a, b):
    return lax.dot_general(a, b, (((1,), (1,)), ((), ())), preferred_element_type=F32)


def wide(ref, start, size):
    return jnp.concatenate([ref[c, start : start + size, :] for c in range(ref.shape[0])], axis=1)


def core_index():
    return lax.axis_index("band") & 1


def one_hot(row, count):
    nodes = lax.broadcasted_iota(I32, (count, row.shape[1]), 0)
    return jnp.where(nodes == row, 1.0, 0.0).astype(BF16)


def code_table(digits, table, core, rows_used):
    width = table.shape[1]
    value = table[...] + 1
    digits[...] = jnp.zeros_like(digits)
    digits[0:5, 0:width] = (value >> 4).astype(F32)
    digits[8:13, 0:width] = (value & 15).astype(F32)
    row = lax.broadcasted_iota(I32, (TILE, 16), 0)
    col = lax.broadcasted_iota(I32, (TILE, 16), 1)
    near = row & 15
    base = jnp.where((row >> 4) == core, 3, 0)
    wanted = (near & 1) * 8 + base + ((near >> 1) & 1)
    total = None
    for k in range(width // LANES):
        pick = jnp.where((col == wanted) & ((near >> 2) == k + rows_used), 1.0, 0.0).astype(BF16)
        part = dot(pick, digits[:, k * LANES : (k + 1) * LANES].astype(BF16))
        total = part if total is None else total + part
    return total


def decode(tile, offset, second):
    row = lax.broadcasted_iota(I32, (8, TILE), 0)
    col = lax.broadcasted_iota(I32, (8, TILE), 1)
    place = offset + (row & 3) * 4 + second * 2
    weight = jnp.where(col == place, 16.0, jnp.where(col == place + 1, 1.0, 0.0))
    return dot(weight.astype(BF16), tile).astype(I32) - 1


def pre_kernel(
    grid_state, big, w_es, w_ed, w_dd, enc_src, enc_dst, dec_src, dec_dst, proc_src, proc_dst,
    payload, enc_recv, dec_recv, latent, digits,
):
    core = core_index()
    channels, nodes = grid_state.shape
    grid_latent = silu(dot_first(grid_state[...], wide(big, 0, channels))).astype(BF16)
    latent[...] = grid_latent
    grid_normed = rms(grid_latent).astype(BF16)
    dec_recv[...] = dot(grid_normed, w_dd[...]).astype(BF16)
    payload[0:nodes, :] = dot(grid_normed, w_es[...]).astype(BF16)
    mesh_count = enc_recv.shape[0]
    mesh_normed = rms(wide(big, big.shape[1] - mesh_count, mesh_count)).astype(BF16)
    enc_recv[...] = dot(mesh_normed, w_ed[...]).astype(BF16)
    for t, table in enumerate((enc_src, enc_dst, dec_src, dec_dst)):
        start = nodes + t * TILE
        payload[start : start + TILE, :] = code_table(digits, table, core, 0).astype(BF16)
    start = nodes + 4 * TILE
    both = code_table(digits, proc_src, core, 0) + code_table(digits, proc_dst, core, 1)
    payload[start : start + TILE, :] = both.astype(BF16)


def add_edges(total, send_t, recv_t, src, dst, send_count, recv_count):
    to = one_hot(dst, recv_count)
    message = silu(dot(send_t, one_hot(src, send_count)) + dot(recv_t, to)).astype(BF16)
    part = dot_last(message, to)
    return part if total is None else total + part


def flat(rows, start, count):
    return jnp.concatenate([rows[start + k : start + k + 1, :] for k in range(count)], axis=1)


def places(core):
    sib = 1 - core
    return (
        ("two", 0, core * 16, 1),
        ("two", 1, 16 - core * 16, 0),
        ("pair", sib, 0, sib),
        ("far", core, 16, core),
    )


def transposed(values):
    return values.astype(F32).T.astype(BF16)


def enc_kernel(
    pair, two, far, recv, enc_src, enc_dst,
    agg, proc_tab, dec_tab,
):
    core = core_index()
    sib = 1 - core
    recv_count = recv.shape[0]
    send_count = pair.shape[1] - TABLES * TILE
    recv_t = transposed(recv[...])
    arrivals = []
    for v, (kind, place, offset, second) in enumerate(places(core)):
        if kind == "two":
            block = two.at[core, place]
        elif kind == "pair":
            block = pair.at[sib]
        else:
            block = far.at[sib]
        lists = [
            decode(block[send_count + t * TILE : send_count + (t + 1) * TILE, :], offset, second)
            for t in range(TABLES)
        ]
        arrivals.append((block, lists))
        dec_tab[0, v] = lists[2]
        dec_tab[1, v] = lists[3]
        proc_tab[v] = lists[4]
    total = None
    for block, lists in arrivals:
        total = add_edges(
            total, transposed(block[0:send_count, :]), recv_t, flat(lists[0], 0, 4), flat(lists[1], 0, 4),
            send_count, recv_count,
        )
    total = add_edges(
        total, transposed(pair[core, 0:send_count, :]), recv_t, enc_src[2:3, :], enc_dst[2:3, :],
        send_count, recv_count,
    )
    agg[...] = jnp.broadcast_to(total.T.astype(BF16)[None], agg.shape)


def source(k):
    return lax.rem(lax.axis_index("chan") + CHANS - k, CHANS)


def arrived(blocks, start, size):
    return jnp.concatenate([block[start : start + size, :] for block in blocks], axis=1)


def columns_at(k):
    return pl.ds(pl.multiple_of(source(k) * LANES, LANES), LANES)


class Rows:
    def __init__(self, ref, start):
        self.ref, self.start = ref, start

    def __getitem__(self, index):
        rows, columns = index
        return self.ref[self.start + rows.start : self.start + rows.stop, columns]


def later_kernel(kernel, start, agg4, state, b0, b1, b2, b3, *rest):
    kernel(agg4, state, *[Rows(b, start) for b in (b0, b1, b2, b3)], *rest)


def layer_kernel(layer, agg4, state, b0, b1, b2, b3, w_proc, *rest):
    node_kernel(True, agg4, state, b0, b1, b2, b3, w_proc.at[layer, 0], w_proc.at[layer, 1], *rest)


def late_kernel(w_enc_out, w_proc, w_out, out):
    depth = w_enc_out.shape[0]
    out[0:depth, :] = w_enc_out[...]
    out[depth : 2 * depth, :] = w_proc[0, 2]
    out[2 * depth : 3 * depth, :] = w_proc[1, 2]
    out[3 * depth : 3 * depth + w_out.shape[0], :] = w_out[...]


def node_kernel(has_recv, agg4, state, b0, b1, b2, b3, w_send, *rest):
    if has_recv:
        w_recv, new_state, send, recv = rest
    else:
        (send,) = rest
    count = agg4.shape[1]
    agg = wide(agg4, 0, count)
    if len(state.shape) == 3:
        first = state.shape[1] - count
        before = jnp.concatenate([state[source(k), first:, :] for k in range(CHANS)], axis=1).astype(F32)
    else:
        before = state[...]
    normed = rms(agg).astype(BF16)
    after = before + dot(normed, arrived((b0, b1, b2, b3), 0, agg.shape[1]))
    normed = rms(after.astype(BF16)).astype(BF16)

    def turned(weight):
        return jnp.concatenate([weight[columns_at(k), :] for k in range(CHANS)], axis=0)

    send[...] = dot(normed, turned(w_send)).astype(BF16)
    if has_recv:
        new_state[...] = after
        recv[...] = dot(normed, turned(w_recv)).astype(BF16)


def proc_kernel(pair, two, far, recv, local_src, local_dst, proc_src, proc_dst, tab, agg):
    core = core_index()
    sib = 1 - core
    count = recv.shape[0]
    recv_t = transposed(recv[...])
    total = None
    for v, block in enumerate((two.at[core, 0], two.at[core, 1], pair.at[sib], far.at[sib])):
        lists = tab[v]
        total = add_edges(
            total, transposed(block[...]), recv_t, lists[0:1, :], lists[1:2, :], count, count
        )
    own_src = jnp.concatenate([local_src[...], proc_src[2:3, :]], axis=1)
    own_dst = jnp.concatenate([local_dst[...], proc_dst[2:3, :]], axis=1)
    total = add_edges(total, transposed(pair[core]), recv_t, own_src, own_dst, count, count)
    agg[...] = jnp.broadcast_to(total.T.astype(BF16)[None], agg.shape)


def dec_kernel(pair, two, far, recv, dec_src, dec_dst, tab, agg):
    core = core_index()
    sib = 1 - core
    recv_count = recv.shape[0]
    send_count = pair.shape[1]
    recv_t = transposed(recv[...])
    total = add_edges(
        None, transposed(pair[core]), recv_t, dec_src[2:3, :], dec_dst[2:3, :], send_count, recv_count
    )
    for v, block in enumerate((two.at[core, 0], two.at[core, 1], pair.at[sib], far.at[sib])):
        total = add_edges(
            total, transposed(block[...]), recv_t, flat(tab[0, v], 0, 4), flat(tab[1, v], 0, 4),
            send_count, recv_count,
        )
    agg[...] = jnp.broadcast_to(total.T.astype(BF16)[None], agg.shape)


def out_kernel(agg4, latent, b0, b1, b2, b3, out):
    combined = jnp.concatenate(
        [agg4[source(k)].astype(F32) + latent[:, columns_at(k)].astype(F32) for k in range(CHANS)], axis=1
    )
    normed = rms(combined).astype(BF16)
    weights = arrived((b0, b1, b2, b3), 0, out.shape[0])
    out[...] = dot_last(weights, normed).astype(BF16)


def call(kernel, out_shapes, *args, scratch=()):
    return pl.pallas_call(
        kernel,
        out_shape=out_shapes,
        in_specs=[pl.BlockSpec(memory_space=pltpu.VMEM)] * len(args),
        out_specs=jax.tree.map(lambda _: pl.BlockSpec(memory_space=pltpu.VMEM), out_shapes),
        scratch_shapes=scratch,
        compiler_params=pltpu.CompilerParams(vmem_limit_bytes=16 * 1024 * 1024),
    )(*args)


def shape(dims, kind=BF16):
    return jax.ShapeDtypeStruct(dims, kind)


def exchange(copies):
    return lax.all_to_all(copies, "chan", 0, 0, tiled=True)


def core_gather(block):
    parts = lax.axis_size("band")
    return lax.all_gather(block, "band", axis_index_groups=[[s, s + 1] for s in range(0, parts, 2)])


def around(block):
    parts = lax.axis_size("band")
    pair = core_gather(block)
    sides = [[s, (s + 1) % parts] for s in range(1, parts, 2)]
    two = lax.all_gather(pair, "band", axis_index_groups=sides)
    near = jnp.where(core_index() == 0, two[0, 1], two[1, 0])
    return pair, two, core_gather(near)


def on_device(
    grid_state, mesh_latent, w_in, w_enc_src, w_enc_dst, w_enc_out, w_proc, w_dec_src, w_dec_dst, w_out,
    enc_src, enc_dst, local_src, local_dst, proc_src, proc_dst, dec_src, dec_dst,
):
    grid_count, channels = grid_state.shape
    mesh_count, width = mesh_latent.shape
    chans = lax.axis_size("chan")
    latent_width = width * chans

    channel_rows = -(-channels // LANES) * LANES
    late_rows = 3 * latent_width + channel_rows
    parts = (jnp.pad(w_in, ((0, channel_rows - channels), (0, 0))), mesh_latent)
    big = exchange(
        jnp.concatenate([jnp.broadcast_to(part[None], (chans,) + part.shape) for part in parts], axis=1)
    )
    late = call(late_kernel, shape((late_rows, width)), w_enc_out, w_proc, w_out.T)
    late, big = lax.optimization_barrier((late, big))
    blocks = [late] + [
        lax.ppermute(late, "chan", [(s, (s + k) % chans) for s in range(chans)]) for k in range(1, chans)
    ]

    payload, recv, dec_recv, grid_latent = call(
        pre_kernel,
        (
            shape((grid_count + TABLES * TILE, width)),
            shape((mesh_count, width)),
            shape((grid_count, width)),
            shape((grid_count, latent_width)),
        ),
        grid_state.T, big, w_enc_src, w_enc_dst, w_dec_dst,
        enc_src, enc_dst, dec_src, dec_dst, proc_src, proc_dst,
        scratch=[pltpu.VMEM((16, enc_src.shape[1]), F32)],
    )
    pair, two, far = around(payload)
    agg, proc_tab, dec_tab = call(
        enc_kernel,
        (shape((chans, mesh_count, width)), shape((4, 8, LANES), I32), shape((2, 4, 8, LANES), I32)),
        pair, two, far, recv, enc_src, enc_dst,
    )
    state = big
    for layer in range(w_proc.shape[0]):
        kernel = functools.partial(layer_kernel, layer)
        state, send, recv = call(
            functools.partial(later_kernel, kernel, layer * latent_width),
            (shape((mesh_count, latent_width), F32), shape((mesh_count, width)), shape((mesh_count, width))),
            exchange(agg), state, *blocks, w_proc,
        )
        pair, two, far = around(send)
        agg = call(
            proc_kernel, shape((chans, mesh_count, width)), pair, two, far, recv,
            local_src, local_dst, proc_src, proc_dst, proc_tab,
        )
    node = functools.partial(later_kernel, functools.partial(node_kernel, False), 2 * latent_width)
    send = call(node, shape((mesh_count, width)), exchange(agg), state, *blocks, w_dec_src)
    pair, two, far = around(send)
    agg = call(
        dec_kernel, shape((chans, grid_count, width)), pair, two, far, dec_recv, dec_src, dec_dst, dec_tab
    )
    last = functools.partial(later_kernel, out_kernel, 3 * latent_width)
    return call(last, shape((channels, grid_count)), exchange(agg), grid_latent, *blocks).T


def solution(mesh):
    placed = (
        P("band", None),
        P("band", "chan"),
        P(None, "chan"),
        P(None, "chan"),
        P(None, "chan"),
        P(None, "chan"),
        P(None, None, None, "chan"),
        P(None, "chan"),
        P(None, "chan"),
        P("chan", None),
    ) + (P("band", None),) * 8
    return jax.shard_map(
        on_device, mesh=mesh, in_specs=placed, out_specs=P("band", None), check_vma=False
    )
```

```python
import functools

import jax
import jax.numpy as jnp
from jax import lax
from jax.experimental import pallas as pl
from jax.experimental.pallas import tpu as pltpu
from jax.sharding import PartitionSpec as P

EPS = 1e-05
F32 = jnp.float32
BF16 = jnp.bfloat16
I32 = jnp.int32
LANES = 128
CHANS = 4
TILE = 32
TABLES = 3


def rms(values):
    values = values.astype(F32)
    return values * lax.rsqrt(jnp.mean(values * values, axis=-1, keepdims=True) + EPS)


def silu(values):
    return 0.5 * values * (1.0 + jnp.tanh(0.5 * values))


def dot(a, b):
    return lax.dot_general(a, b, (((1,), (0,)), ((), ())), preferred_element_type=F32)


def dot_first(a, b):
    return lax.dot_general(a, b, (((0,), (0,)), ((), ())), preferred_element_type=F32)


def dot_last(a, b):
    return lax.dot_general(a, b, (((1,), (1,)), ((), ())), preferred_element_type=F32)


def wide(ref, start, size):
    return jnp.concatenate([ref[c, start : start + size, :] for c in range(ref.shape[0])], axis=1)


def core_index():
    return lax.axis_index("band") & 1


def one_hot(row, count):
    nodes = lax.broadcasted_iota(I32, (count, row.shape[1]), 0).astype(jnp.int16)
    hit = nodes == row.astype(jnp.int16)
    return jnp.where(hit, jnp.ones((), BF16), jnp.zeros((), BF16))


def code_table(digits, table, core, rows_used):
    width = table.shape[1]
    value = table[...] + 1
    digits[...] = jnp.zeros_like(digits)
    digits[0:5, 0:width] = (value >> 4).astype(F32)
    digits[8:13, 0:width] = (value & 15).astype(F32)
    row = lax.broadcasted_iota(I32, (TILE, 16), 0)
    col = lax.broadcasted_iota(I32, (TILE, 16), 1)
    near = row & 15
    base = jnp.where((row >> 4) == core, 3, 0)
    wanted = (near & 1) * 8 + base + ((near >> 1) & 1)
    total = None
    for k in range(width // LANES):
        pick = jnp.where((col == wanted) & ((near >> 2) == k + rows_used), 1.0, 0.0).astype(BF16)
        part = dot(pick, digits[:, k * LANES : (k + 1) * LANES].astype(BF16))
        total = part if total is None else total + part
    return total


def decode(tile, offset, second):
    row = lax.broadcasted_iota(I32, (8, TILE), 0)
    col = lax.broadcasted_iota(I32, (8, TILE), 1)
    place = offset + (row & 3) * 4 + second * 2
    weight = jnp.where(col == place, 16.0, jnp.where(col == place + 1, 1.0, 0.0))
    return dot(weight.astype(BF16), tile).astype(I32) - 1


def pre_kernel(
    grid_state, big, w_es, w_ed, w_dd, enc_src, enc_dst, proc_src, proc_dst,
    payload, enc_recv, dec_recv, latent, digits,
):
    core = core_index()
    channels, nodes = grid_state.shape
    grid_latent = silu(dot_first(grid_state[...], wide(big, enc_recv.shape[0], channels))).astype(BF16)
    latent[...] = grid_latent
    grid_normed = rms(grid_latent).astype(BF16)
    dec_recv[...] = dot(grid_normed, w_dd[...]).astype(BF16)
    payload[0:nodes, :] = dot(grid_normed, w_es[...]).astype(BF16)
    mesh_count = enc_recv.shape[0]
    mesh_normed = rms(wide(big, 0, mesh_count)).astype(BF16)
    enc_recv[...] = dot(mesh_normed, w_ed[...]).astype(BF16)
    for t, table in enumerate((enc_src, enc_dst)):
        start = nodes + t * TILE
        payload[start : start + TILE, :] = code_table(digits, table, core, 0).astype(BF16)
    start = nodes + 2 * TILE
    both = code_table(digits, proc_src, core, 0) + code_table(digits, proc_dst, core, 1)
    payload[start : start + TILE, :] = both.astype(BF16)


def add_edges(total, send_t, recv_t, src, dst, send_count, recv_count):
    to = one_hot(dst, recv_count)
    message = silu(dot(send_t, one_hot(src, send_count)) + dot(recv_t, to)).astype(BF16)
    part = dot_last(message, to)
    return part if total is None else total + part


def flat(rows, start, count):
    return jnp.concatenate([rows[start + k : start + k + 1, :] for k in range(count)], axis=1)


def places(pair, two, far, core):
    sib = 1 - core
    return (
        (two.at[core, 0], core * 16, 1),
        (two.at[core, 1], 16 - core * 16, 0),
        (pair.at[sib], 0, sib),
        (far.at[sib], 16, core),
    )


def transposed(values):
    return values.astype(F32).T.astype(BF16)


def enc_kernel(
    pair, two, far, recv, enc_src, enc_dst,
    agg, proc_tab,
):
    core = core_index()
    recv_count = recv.shape[0]
    send_count = pair.shape[1] - TABLES * TILE
    recv_t = transposed(recv[...])
    arrivals = []
    for v, (block, offset, second) in enumerate(places(pair, two, far, core)):
        lists = [
            decode(block[send_count + t * TILE : send_count + (t + 1) * TILE, :], offset, second)
            for t in range(TABLES)
        ]
        arrivals.append((block, lists))
        proc_tab[v] = lists[2]
    total = None
    for block, lists in arrivals:
        total = add_edges(
            total, transposed(block[0:send_count, :]), recv_t, flat(lists[0], 0, 4), flat(lists[1], 0, 4),
            send_count, recv_count,
        )
    total = add_edges(
        total, transposed(pair[core, 0:send_count, :]), recv_t, enc_src[2:3, :], enc_dst[2:3, :],
        send_count, recv_count,
    )
    agg[...] = jnp.broadcast_to(total.T.astype(BF16)[None], agg.shape)


def source(k):
    return lax.rem(lax.axis_index("chan") + CHANS - k, CHANS)


def arrived(blocks, start, size):
    return jnp.concatenate([block[start : start + size, :] for block in blocks], axis=1)


def columns_at(k):
    return pl.ds(pl.multiple_of(source(k) * LANES, LANES), LANES)


class Rows:
    def __init__(self, ref, start):
        self.ref, self.start = ref, start

    def __getitem__(self, index):
        rows, columns = index
        return self.ref[self.start + rows.start : self.start + rows.stop, columns]


def later_kernel(kernel, start, agg4, state, b0, b1, b2, b3, *rest):
    kernel(agg4, state, *[Rows(b, start) for b in (b0, b1, b2, b3)], *rest)


def layer_kernel(layer, agg4, state, b0, b1, b2, b3, w_proc, *rest):
    node_kernel(True, agg4, state, b0, b1, b2, b3, w_proc.at[layer, 0], w_proc.at[layer, 1], *rest)


def late_kernel(w_enc_out, w_proc, w_out, *rest):
    out = rest[-1]
    depth = w_enc_out.shape[0]
    out[0:depth, :] = w_enc_out[...]
    out[depth : 2 * depth, :] = w_proc[0, 2]
    out[2 * depth : 3 * depth, :] = w_proc[1, 2]
    out[3 * depth : 3 * depth + w_out.shape[0], :] = w_out[...]


def node_kernel(has_recv, agg4, state, b0, b1, b2, b3, w_send, *rest):
    if has_recv:
        w_recv, new_state, send, recv = rest
    else:
        dec_src, dec_dst, send, digits = rest
        core = core_index()
        for t, table in enumerate((dec_src, dec_dst)):
            start = send.shape[0] - (2 - t) * TILE
            send[start : start + TILE, :] = code_table(digits, table, core, 0).astype(BF16)
    count = agg4.shape[1]
    agg = wide(agg4, 0, count)
    if len(state.shape) == 3:
        before = jnp.concatenate([state[source(k), 0:count, :] for k in range(CHANS)], axis=1).astype(F32)
    else:
        before = state[...]
    normed = rms(agg).astype(BF16)
    after = before + dot(normed, arrived((b0, b1, b2, b3), 0, agg.shape[1]))
    normed = rms(after.astype(BF16)).astype(BF16)

    def turned(weight):
        return jnp.concatenate([weight[columns_at(k), :] for k in range(CHANS)], axis=0)

    send[0:count, :] = dot(normed, turned(w_send)).astype(BF16)
    if has_recv:
        new_state[...] = after
        recv[...] = dot(normed, turned(w_recv)).astype(BF16)


def proc_kernel(pair, two, far, recv, local_src, local_dst, proc_src, proc_dst, tab, agg):
    core = core_index()
    sib = 1 - core
    count = recv.shape[0]
    recv_t = transposed(recv[...])
    total = None
    for v, block in enumerate((two.at[core, 0], two.at[core, 1], pair.at[sib], far.at[sib])):
        lists = tab[v]
        total = add_edges(
            total, transposed(block[...]), recv_t, lists[0:1, :], lists[1:2, :], count, count
        )
    own_src = jnp.concatenate([local_src[...], proc_src[2:3, :]], axis=1)
    own_dst = jnp.concatenate([local_dst[...], proc_dst[2:3, :]], axis=1)
    total = add_edges(total, transposed(pair[core]), recv_t, own_src, own_dst, count, count)
    agg[...] = jnp.broadcast_to(total.T.astype(BF16)[None], agg.shape)


def dec_kernel(pair, two, far, recv, dec_src, dec_dst, agg):
    core = core_index()
    recv_count = recv.shape[0]
    send_count = pair.shape[1] - 2 * TILE
    recv_t = transposed(recv[...])
    total = add_edges(
        None, transposed(pair[core, 0:send_count, :]), recv_t, dec_src[2:3, :], dec_dst[2:3, :],
        send_count, recv_count,
    )
    for block, offset, second in places(pair, two, far, core):
        src, dst = [
            flat(decode(block[start : start + TILE, :], offset, second), 0, 4)
            for start in (send_count, send_count + TILE)
        ]
        total = add_edges(
            total, transposed(block[0:send_count, :]), recv_t, src, dst, send_count, recv_count
        )
    agg[...] = jnp.broadcast_to(total.T.astype(BF16)[None], agg.shape)


def out_kernel(agg4, latent, b0, b1, b2, b3, out):
    combined = jnp.concatenate(
        [agg4[source(k)].astype(F32) + latent[:, columns_at(k)].astype(F32) for k in range(CHANS)], axis=1
    )
    normed = rms(combined).astype(BF16)
    weights = arrived((b0, b1, b2, b3), 0, out.shape[0])
    out[...] = dot_last(weights, normed).astype(BF16)


def call(kernel, out_shapes, *args, scratch=()):
    return pl.pallas_call(
        kernel,
        out_shape=out_shapes,
        in_specs=[pl.BlockSpec(memory_space=pltpu.VMEM)] * len(args),
        out_specs=jax.tree.map(lambda _: pl.BlockSpec(memory_space=pltpu.VMEM), out_shapes),
        scratch_shapes=scratch,
        compiler_params=pltpu.CompilerParams(vmem_limit_bytes=16 * 1024 * 1024),
    )(*args)


def shape(dims, kind=BF16):
    return jax.ShapeDtypeStruct(dims, kind)


def exchange(copies):
    return lax.all_to_all(copies, "chan", 0, 0, tiled=True)


def core_gather(block):
    parts = lax.axis_size("band")
    return lax.all_gather(block, "band", axis_index_groups=[[s, s + 1] for s in range(0, parts, 2)])


def around(block):
    parts = lax.axis_size("band")
    pair = core_gather(block)
    sides = [[s, (s + 1) % parts] for s in range(1, parts, 2)]
    two = lax.all_gather(pair, "band", axis_index_groups=sides)
    near = jnp.where(core_index() == 0, two[0, 1], two[1, 0])
    return pair, two, core_gather(near)


def on_device(
    grid_state, mesh_latent, w_in, w_enc_src, w_enc_dst, w_enc_out, w_proc, w_dec_src, w_dec_dst, w_out,
    enc_src, enc_dst, local_src, local_dst, proc_src, proc_dst, dec_src, dec_dst,
):
    grid_count, channels = grid_state.shape
    mesh_count, width = mesh_latent.shape
    chans = lax.axis_size("chan")
    latent_width = width * chans

    channel_rows = -(-channels // LANES) * LANES
    late_rows = 3 * latent_width + channel_rows
    early = jnp.concatenate(
        [jnp.broadcast_to(part[None], (chans,) + part.shape) for part in (mesh_latent, w_in)], axis=1
    )
    early, w_enc_out = lax.optimization_barrier((early, w_enc_out))
    big = exchange(early)
    soon = (grid_state.T, w_enc_src, w_enc_dst, w_dec_dst, enc_src, enc_dst, proc_src, proc_dst)
    late = call(late_kernel, shape((late_rows, width)), w_enc_out, w_proc, w_out.T, *soon)
    blocks = [late] + [
        lax.ppermute(late, "chan", [(s, (s + k) % chans) for s in range(chans)]) for k in range(1, chans)
    ]

    payload, recv, dec_recv, grid_latent = call(
        pre_kernel,
        (
            shape((grid_count + TABLES * TILE, width)),
            shape((mesh_count, width)),
            shape((grid_count, width)),
            shape((grid_count, latent_width)),
        ),
        soon[0], big, *soon[1:],
        scratch=[pltpu.VMEM((16, enc_src.shape[1]), F32)],
    )
    pair, two, far = around(payload)
    agg, proc_tab = call(
        enc_kernel,
        (shape((chans, mesh_count, width)), shape((4, 8, LANES), I32)),
        pair, two, far, recv, enc_src, enc_dst,
    )
    agg, *blocks = lax.optimization_barrier((agg, *blocks))
    state = big
    for layer in range(w_proc.shape[0]):
        kernel = functools.partial(layer_kernel, layer)
        state, send, recv = call(
            functools.partial(later_kernel, kernel, layer * latent_width),
            (shape((mesh_count, latent_width), F32), shape((mesh_count, width)), shape((mesh_count, width))),
            exchange(agg), state, *blocks, w_proc,
        )
        pair, two, far = around(send)
        agg = call(
            proc_kernel, shape((chans, mesh_count, width)), pair, two, far, recv,
            local_src, local_dst, proc_src, proc_dst, proc_tab,
        )
    node = functools.partial(later_kernel, functools.partial(node_kernel, False), 2 * latent_width)
    send = call(
        node, shape((mesh_count + 2 * TILE, width)),
        exchange(agg), state, *blocks, w_dec_src, dec_src, dec_dst,
        scratch=[pltpu.VMEM((16, dec_src.shape[1]), F32)],
    )
    pair, two, far = around(send)
    agg = call(
        dec_kernel, shape((chans, grid_count, width)), pair, two, far, dec_recv, dec_src, dec_dst
    )
    last = functools.partial(later_kernel, out_kernel, 3 * latent_width)
    return call(last, shape((channels, grid_count)), exchange(agg), grid_latent, *blocks).T


def solution(mesh):
    placed = (
        P("band", None),
        P("band", "chan"),
        P(None, "chan"),
        P(None, "chan"),
        P(None, "chan"),
        P(None, "chan"),
        P(None, None, None, "chan"),
        P(None, "chan"),
        P(None, "chan"),
        P("chan", None),
    ) + (P("band", None),) * 8
    return jax.shard_map(
        on_device, mesh=mesh, in_specs=placed, out_specs=P("band", None), check_vma=False
    )
```

```python
import functools

import jax
import jax.numpy as jnp
from jax import lax
from jax.experimental import pallas as pl
from jax.experimental.pallas import tpu as pltpu
from jax.sharding import PartitionSpec as P

EPS = 1e-05
F32 = jnp.float32
BF16 = jnp.bfloat16
I32 = jnp.int32
LANES = 128
CHANS = 4
TILE = 32
TABLES = 3


def rms(values):
    values = values.astype(F32)
    return values * lax.rsqrt(jnp.mean(values * values, axis=-1, keepdims=True) + EPS)


def silu(values):
    return 0.5 * values * (1.0 + jnp.tanh(0.5 * values))


def dot(a, b):
    return lax.dot_general(a, b, (((1,), (0,)), ((), ())), preferred_element_type=F32)


def dot_first(a, b):
    return lax.dot_general(a, b, (((0,), (0,)), ((), ())), preferred_element_type=F32)


def dot_last(a, b):
    return lax.dot_general(a, b, (((1,), (1,)), ((), ())), preferred_element_type=F32)


def wide(ref, start, size):
    return jnp.concatenate([ref[c, start : start + size, :] for c in range(ref.shape[0])], axis=1)


def core_index():
    return lax.axis_index("band") & 1


def one_hot(row, count):
    nodes = lax.broadcasted_iota(I32, (count, row.shape[1]), 0).astype(jnp.int16)
    hit = nodes == row.astype(jnp.int16)
    return jnp.where(hit, jnp.ones((), BF16), jnp.zeros((), BF16))


def code_table(digits, table, core, rows_used):
    width = table.shape[1]
    value = table[...] + 1
    digits[...] = jnp.zeros_like(digits)
    digits[0:5, 0:width] = (value >> 4).astype(F32)
    digits[8:13, 0:width] = (value & 15).astype(F32)
    row = lax.broadcasted_iota(I32, (TILE, 16), 0)
    col = lax.broadcasted_iota(I32, (TILE, 16), 1)
    near = row & 15
    base = jnp.where((row >> 4) == core, 3, 0)
    wanted = (near & 1) * 8 + base + ((near >> 1) & 1)
    total = None
    for k in range(width // LANES):
        pick = jnp.where((col == wanted) & ((near >> 2) == k + rows_used), 1.0, 0.0).astype(BF16)
        part = dot(pick, digits[:, k * LANES : (k + 1) * LANES].astype(BF16))
        total = part if total is None else total + part
    return total


def decode(tile, offset, second):
    row = lax.broadcasted_iota(I32, (8, TILE), 0)
    col = lax.broadcasted_iota(I32, (8, TILE), 1)
    place = offset + (row & 3) * 4 + second * 2
    weight = jnp.where(col == place, 16.0, jnp.where(col == place + 1, 1.0, 0.0))
    return dot(weight.astype(BF16), tile).astype(I32) - 1


def pre_kernel(
    grid_state, big, w_es, enc_src, enc_dst, proc_src, proc_dst, payload, latent, digits,
):
    core = core_index()
    channels, nodes = grid_state.shape
    first = big.shape[1] - channels
    grid_latent = silu(dot_first(grid_state[...], wide(big, first, channels))).astype(BF16)
    latent[...] = grid_latent
    payload[0:nodes, :] = dot(rms(grid_latent).astype(BF16), w_es[...]).astype(BF16)
    for t, table in enumerate((enc_src, enc_dst)):
        start = nodes + t * TILE
        payload[start : start + TILE, :] = code_table(digits, table, core, 0).astype(BF16)
    start = nodes + 2 * TILE
    both = code_table(digits, proc_src, core, 0) + code_table(digits, proc_dst, core, 1)
    payload[start : start + TILE, :] = both.astype(BF16)


def add_edges(total, send_t, recv_t, src, dst, send_count, recv_count):
    to = one_hot(dst, recv_count)
    message = silu(dot(send_t, one_hot(src, send_count)) + dot(recv_t, to)).astype(BF16)
    part = dot_last(message, to)
    return part if total is None else total + part


def flat(rows, start, count):
    return jnp.concatenate([rows[start + k : start + k + 1, :] for k in range(count)], axis=1)


def places(pair, two, far, core):
    sib = 1 - core
    return (
        (two.at[core, 0], core * 16, 1),
        (two.at[core, 1], 16 - core * 16, 0),
        (pair.at[sib], 0, sib),
        (far.at[sib], 16, core),
    )


def transposed(values):
    return values.astype(F32).T.astype(BF16)


def enc_kernel(
    pair, two, far, big, w_ed, enc_src, enc_dst,
    agg, proc_tab,
):
    core = core_index()
    recv_count = agg.shape[1]
    send_count = pair.shape[1] - TABLES * TILE
    recv = dot(rms(wide(big, 0, recv_count)).astype(BF16), w_ed[...])
    recv_t = recv.T.astype(BF16)
    arrivals = []
    for v, (block, offset, second) in enumerate(places(pair, two, far, core)):
        lists = [
            decode(block[send_count + t * TILE : send_count + (t + 1) * TILE, :], offset, second)
            for t in range(TABLES)
        ]
        arrivals.append((block, lists))
        proc_tab[v] = lists[2]
    total = None
    for block, lists in arrivals:
        total = add_edges(
            total, transposed(block[0:send_count, :]), recv_t, flat(lists[0], 0, 4), flat(lists[1], 0, 4),
            send_count, recv_count,
        )
    total = add_edges(
        total, transposed(pair[core, 0:send_count, :]), recv_t, enc_src[2:3, :], enc_dst[2:3, :],
        send_count, recv_count,
    )
    agg[...] = jnp.broadcast_to(total.T.astype(BF16)[None], agg.shape)


def source(k):
    return lax.rem(lax.axis_index("chan") + CHANS - k, CHANS)


def arrived(blocks, start, size):
    return jnp.concatenate([block[start : start + size, :] for block in blocks], axis=1)


def columns_at(k):
    return pl.ds(pl.multiple_of(source(k) * LANES, LANES), LANES)


class Rows:
    def __init__(self, ref, start):
        self.ref, self.start = ref, start

    def __getitem__(self, index):
        rows, columns = index
        return self.ref[self.start + rows.start : self.start + rows.stop, columns]


def later_kernel(kernel, start, agg4, state, b0, b1, b2, b3, *rest):
    kernel(agg4, state, *[Rows(b, start) for b in (b0, b1, b2, b3)], *rest)


def layer_kernel(layer, agg4, state, b0, b1, b2, b3, w_proc, *rest):
    node_kernel(True, agg4, state, b0, b1, b2, b3, w_proc.at[layer, 0], w_proc.at[layer, 1], *rest)


def late_kernel(w_enc_out, w_proc, w_out, *rest):
    out = rest[-1]
    depth = w_enc_out.shape[0]
    out[0:depth, :] = w_enc_out[...]
    out[depth : 2 * depth, :] = w_proc[0, 2]
    out[2 * depth : 3 * depth, :] = w_proc[1, 2]
    out[3 * depth : 3 * depth + w_out.shape[0], :] = w_out[...]


def node_kernel(has_recv, agg4, state, b0, b1, b2, b3, w_send, *rest):
    if has_recv:
        w_recv, new_state, send, recv = rest
    else:
        dec_src, dec_dst, send, digits = rest
        core = core_index()
        for t, table in enumerate((dec_src, dec_dst)):
            start = send.shape[0] - (2 - t) * TILE
            send[start : start + TILE, :] = code_table(digits, table, core, 0).astype(BF16)
    count = agg4.shape[1]
    agg = wide(agg4, 0, count)
    if len(state.shape) == 3:
        before = jnp.concatenate([state[source(k), 0:count, :] for k in range(CHANS)], axis=1).astype(F32)
    else:
        before = state[...]
    normed = rms(agg).astype(BF16)
    after = before + dot(normed, arrived((b0, b1, b2, b3), 0, agg.shape[1]))
    normed = rms(after.astype(BF16)).astype(BF16)

    def turned(weight):
        return jnp.concatenate([weight[columns_at(k), :] for k in range(CHANS)], axis=0)

    send[0:count, :] = dot(normed, turned(w_send)).astype(BF16)
    if has_recv:
        new_state[...] = after
        recv[...] = dot(normed, turned(w_recv)).astype(BF16)


def proc_kernel(pair, two, far, recv, local_src, local_dst, proc_src, proc_dst, tab, agg):
    core = core_index()
    sib = 1 - core
    count = recv.shape[0]
    recv_t = transposed(recv[...])
    total = None
    for v, block in enumerate((two.at[core, 0], two.at[core, 1], pair.at[sib], far.at[sib])):
        lists = tab[v]
        total = add_edges(
            total, transposed(block[...]), recv_t, lists[0:1, :], lists[1:2, :], count, count
        )
    own_src = jnp.concatenate([local_src[...], proc_src[2:3, :]], axis=1)
    own_dst = jnp.concatenate([local_dst[...], proc_dst[2:3, :]], axis=1)
    total = add_edges(total, transposed(pair[core]), recv_t, own_src, own_dst, count, count)
    agg[...] = jnp.broadcast_to(total.T.astype(BF16)[None], agg.shape)


def dec_kernel(pair, two, far, latent, w_dd, dec_src, dec_dst, agg):
    core = core_index()
    recv_count = agg.shape[1]
    send_count = pair.shape[1] - 2 * TILE
    recv_t = dot(rms(latent[...]).astype(BF16), w_dd[...]).T.astype(BF16)
    arrivals = [(pair.at[core], dec_src[2:3, :], dec_dst[2:3, :])]
    for block, offset, second in places(pair, two, far, core):
        src, dst = [
            flat(decode(block[start : start + TILE, :], offset, second), 0, 4)
            for start in (send_count, send_count + TILE)
        ]
        arrivals.append((block, src, dst))
    total = None
    for block, src, dst in arrivals:
        total = add_edges(
            total, transposed(block[0:send_count, :]), recv_t, src, dst, send_count, recv_count
        )
    agg[...] = jnp.broadcast_to(total.T.astype(BF16)[None], agg.shape)


def out_kernel(agg4, latent, b0, b1, b2, b3, out):
    combined = jnp.concatenate(
        [agg4[source(k)].astype(F32) + latent[:, columns_at(k)].astype(F32) for k in range(CHANS)], axis=1
    )
    normed = rms(combined).astype(BF16)
    weights = arrived((b0, b1, b2, b3), 0, out.shape[0])
    out[...] = dot_last(weights, normed).astype(BF16)


def call(kernel, out_shapes, *args, scratch=()):
    return pl.pallas_call(
        kernel,
        out_shape=out_shapes,
        in_specs=[pl.BlockSpec(memory_space=pltpu.VMEM)] * len(args),
        out_specs=jax.tree.map(lambda _: pl.BlockSpec(memory_space=pltpu.VMEM), out_shapes),
        scratch_shapes=scratch,
        compiler_params=pltpu.CompilerParams(vmem_limit_bytes=16 * 1024 * 1024),
    )(*args)


def shape(dims, kind=BF16):
    return jax.ShapeDtypeStruct(dims, kind)


def exchange(copies):
    return lax.all_to_all(copies, "chan", 0, 0, tiled=True)


def core_gather(block):
    parts = lax.axis_size("band")
    return lax.all_gather(block, "band", axis_index_groups=[[s, s + 1] for s in range(0, parts, 2)])


def around(block):
    parts = lax.axis_size("band")
    pair = core_gather(block)
    sides = [[s, (s + 1) % parts] for s in range(1, parts, 2)]
    two = lax.all_gather(pair, "band", axis_index_groups=sides)
    near = jnp.where(core_index() == 0, two[0, 1], two[1, 0])
    return pair, two, core_gather(near)


def on_device(
    grid_state, mesh_latent, w_in, w_enc_src, w_enc_dst, w_enc_out, w_proc, w_dec_src, w_dec_dst, w_out,
    enc_src, enc_dst, local_src, local_dst, proc_src, proc_dst, dec_src, dec_dst,
):
    grid_count, channels = grid_state.shape
    mesh_count, width = mesh_latent.shape
    chans = lax.axis_size("chan")
    latent_width = width * chans

    channel_rows = -(-channels // LANES) * LANES
    late_rows = 3 * latent_width + channel_rows
    early = jnp.concatenate(
        [jnp.broadcast_to(part[None], (chans,) + part.shape) for part in (mesh_latent, w_in)], axis=1
    )
    early, w_enc_out = lax.optimization_barrier((early, w_enc_out))
    big = exchange(early)
    soon = (grid_state.T, w_enc_src, enc_src, enc_dst, proc_src, proc_dst)
    late = call(late_kernel, shape((late_rows, width)), w_enc_out, w_proc, w_out.T, *soon)
    blocks = [late] + [
        lax.ppermute(late, "chan", [(s, (s + k) % chans) for s in range(chans)]) for k in range(1, chans)
    ]

    payload, grid_latent = call(
        pre_kernel,
        (shape((grid_count + TABLES * TILE, width)), shape((grid_count, latent_width))),
        soon[0], big, *soon[1:],
        scratch=[pltpu.VMEM((16, enc_src.shape[1]), F32)],
    )
    pair, two, far = around(payload)
    agg, proc_tab = call(
        enc_kernel,
        (shape((chans, mesh_count, width)), shape((4, 8, LANES), I32)),
        pair, two, far, big, w_enc_dst, enc_src, enc_dst,
    )
    agg, *blocks = lax.optimization_barrier((agg, *blocks))
    state = big
    for layer in range(w_proc.shape[0]):
        kernel = functools.partial(layer_kernel, layer)
        state, send, recv = call(
            functools.partial(later_kernel, kernel, layer * latent_width),
            (shape((mesh_count, latent_width), F32), shape((mesh_count, width)), shape((mesh_count, width))),
            exchange(agg), state, *blocks, w_proc,
        )
        pair, two, far = around(send)
        agg = call(
            proc_kernel, shape((chans, mesh_count, width)), pair, two, far, recv,
            local_src, local_dst, proc_src, proc_dst, proc_tab,
        )
    node = functools.partial(later_kernel, functools.partial(node_kernel, False), 2 * latent_width)
    send = call(
        node, shape((mesh_count + 2 * TILE, width)),
        exchange(agg), state, *blocks, w_dec_src, dec_src, dec_dst,
        scratch=[pltpu.VMEM((16, dec_src.shape[1]), F32)],
    )
    pair, two, far = around(send)
    agg = call(
        dec_kernel, shape((chans, grid_count, width)), pair, two, far, grid_latent, w_dec_dst, dec_src, dec_dst
    )
    last = functools.partial(later_kernel, out_kernel, 3 * latent_width)
    return call(last, shape((channels, grid_count)), exchange(agg), grid_latent, *blocks).T


def solution(mesh):
    placed = (
        P("band", None),
        P("band", "chan"),
        P(None, "chan"),
        P(None, "chan"),
        P(None, "chan"),
        P(None, "chan"),
        P(None, None, None, "chan"),
        P(None, "chan"),
        P(None, "chan"),
        P("chan", None),
    ) + (P("band", None),) * 8
    return jax.shard_map(
        on_device, mesh=mesh, in_specs=placed, out_specs=P("band", None), check_vma=False
    )
```

```python
import functools

import jax
import jax.numpy as jnp
from jax import lax
from jax.experimental import pallas as pl
from jax.experimental.pallas import tpu as pltpu
from jax.sharding import PartitionSpec as P

EPS = 1e-05
F32 = jnp.float32
BF16 = jnp.bfloat16
I32 = jnp.int32
LANES = 128
CHANS = 4
TILE = 32
TABLES = 3


def rms(values):
    values = values.astype(F32)
    return values * lax.rsqrt(jnp.mean(values * values, axis=-1, keepdims=True) + EPS)


def silu(values):
    return 0.5 * values * (1.0 + jnp.tanh(0.5 * values))


def dot(a, b):
    return lax.dot_general(a, b, (((1,), (0,)), ((), ())), preferred_element_type=F32)


def dot_first(a, b):
    return lax.dot_general(a, b, (((0,), (0,)), ((), ())), preferred_element_type=F32)


def dot_last(a, b):
    return lax.dot_general(a, b, (((1,), (1,)), ((), ())), preferred_element_type=F32)


def wide(ref, start, size):
    return jnp.concatenate([ref[c, start : start + size, :] for c in range(ref.shape[0])], axis=1)


def core_index():
    return lax.axis_index("band") & 1


def one_hot(row, count):
    nodes = lax.broadcasted_iota(I32, (count, row.shape[1]), 0).astype(jnp.int16)
    hit = nodes == row.astype(jnp.int16)
    return jnp.where(hit, jnp.ones((), BF16), jnp.zeros((), BF16))


def code_table(digits, table, core, rows_used):
    width = table.shape[1]
    value = table[...] + 1
    digits[...] = jnp.zeros_like(digits)
    digits[0:5, 0:width] = (value >> 4).astype(F32)
    digits[8:13, 0:width] = (value & 15).astype(F32)
    row = lax.broadcasted_iota(I32, (TILE, 16), 0)
    col = lax.broadcasted_iota(I32, (TILE, 16), 1)
    near = row & 15
    base = jnp.where((row >> 4) == core, 3, 0)
    wanted = (near & 1) * 8 + base + ((near >> 1) & 1)
    total = None
    for k in range(width // LANES):
        pick = jnp.where((col == wanted) & ((near >> 2) == k + rows_used), 1.0, 0.0).astype(BF16)
        part = dot(pick, digits[:, k * LANES : (k + 1) * LANES].astype(BF16))
        total = part if total is None else total + part
    return total


def decode(tile, offset, second):
    row = lax.broadcasted_iota(I32, (8, TILE), 0)
    col = lax.broadcasted_iota(I32, (8, TILE), 1)
    place = offset + (row & 3) * 4 + second * 2
    weight = jnp.where(col == place, 16.0, jnp.where(col == place + 1, 1.0, 0.0))
    return dot(weight.astype(BF16), tile).astype(I32) - 1


def pre_kernel(
    grid_state, big, w_es, enc_src, enc_dst, proc_src, proc_dst, payload, latent, digits,
):
    core = core_index()
    channels, nodes = grid_state.shape
    first = big.shape[1] - channels
    grid_latent = silu(dot_first(grid_state[...], wide(big, first, channels))).astype(BF16)
    latent[...] = grid_latent
    payload[0:nodes, :] = dot(rms(grid_latent).astype(BF16), w_es[...]).astype(BF16)
    for t, table in enumerate((enc_src, enc_dst)):
        start = nodes + t * TILE
        payload[start : start + TILE, :] = code_table(digits, table, core, 0).astype(BF16)
    start = nodes + 2 * TILE
    both = code_table(digits, proc_src, core, 0) + code_table(digits, proc_dst, core, 1)
    payload[start : start + TILE, :] = both.astype(BF16)


def add_edges(total, send_t, recv_t, src, dst, send_count, recv_count):
    to = one_hot(dst, recv_count)
    ends = jnp.concatenate([one_hot(src, send_count), to], axis=0)
    message = silu(dot(jnp.concatenate([send_t, recv_t], axis=1), ends)).astype(BF16)
    part = dot_last(message, to)
    return part if total is None else total + part


def flat(rows, start, count):
    return jnp.concatenate([rows[start + k : start + k + 1, :] for k in range(count)], axis=1)


def places(pair, two, far, core):
    sib = 1 - core
    return (
        (two.at[core, 0], core * 16, 1),
        (two.at[core, 1], 16 - core * 16, 0),
        (pair.at[sib], 0, sib),
        (far.at[sib], 16, core),
    )


def transposed(values):
    return values.astype(F32).T.astype(BF16)


def enc_kernel(
    pair, two, far, big, w_ed, enc_src, enc_dst, proc_src, proc_dst, local_src, local_dst,
    agg, proc_tab, inner,
):
    core = core_index()
    recv_count = agg.shape[1]
    send_count = pair.shape[1] - TABLES * TILE
    count = local_src.shape[1]
    for i, (local, proc) in enumerate(((local_src, proc_src), (local_dst, proc_dst))):
        inner[i : i + 1, 0:count] = local[...]
        inner[i : i + 1, count:] = proc[2:3, :]
    recv = dot(rms(wide(big, 0, recv_count)).astype(BF16), w_ed[...])
    recv_t = recv.T.astype(BF16)
    arrivals = []
    for v, (block, offset, second) in enumerate(places(pair, two, far, core)):
        lists = [
            decode(block[send_count + t * TILE : send_count + (t + 1) * TILE, :], offset, second)
            for t in range(TABLES)
        ]
        arrivals.append((block, lists))
        proc_tab[v] = lists[2]
    total = None
    for block, lists in arrivals:
        total = add_edges(
            total, transposed(block[0:send_count, :]), recv_t, flat(lists[0], 0, 4), flat(lists[1], 0, 4),
            send_count, recv_count,
        )
    total = add_edges(
        total, transposed(pair[core, 0:send_count, :]), recv_t, enc_src[2:3, :], enc_dst[2:3, :],
        send_count, recv_count,
    )
    agg[...] = jnp.broadcast_to(total.T.astype(BF16)[None], agg.shape)


def source(k):
    return lax.rem(lax.axis_index("chan") + CHANS - k, CHANS)


def arrived(blocks, start, size):
    return jnp.concatenate([block[start : start + size, :] for block in blocks], axis=1)


def columns_at(k):
    return pl.ds(pl.multiple_of(source(k) * LANES, LANES), LANES)


class Rows:
    def __init__(self, ref, start):
        self.ref, self.start = ref, start

    def __getitem__(self, index):
        rows, columns = index
        return self.ref[self.start + rows.start : self.start + rows.stop, columns]


def later_kernel(kernel, start, agg4, state, b0, b1, b2, b3, *rest):
    kernel(agg4, state, *[Rows(b, start) for b in (b0, b1, b2, b3)], *rest)


def layer_kernel(layer, agg4, state, b0, b1, b2, b3, w_proc, *rest):
    node_kernel(True, agg4, state, b0, b1, b2, b3, w_proc.at[layer, 0], w_proc.at[layer, 1], *rest)


def late_kernel(w_enc_out, w_proc, w_out, *rest):
    out = rest[-1]
    depth = w_enc_out.shape[0]
    out[0:depth, :] = w_enc_out[...]
    out[depth : 2 * depth, :] = w_proc[0, 2]
    out[2 * depth : 3 * depth, :] = w_proc[1, 2]
    out[3 * depth : 3 * depth + w_out.shape[0], :] = w_out[...]


def node_kernel(has_recv, agg4, state, b0, b1, b2, b3, w_send, *rest):
    if has_recv:
        w_recv, new_state, send, recv = rest
    else:
        dec_src, dec_dst, send, digits = rest
        core = core_index()
        for t, table in enumerate((dec_src, dec_dst)):
            start = send.shape[0] - (2 - t) * TILE
            send[start : start + TILE, :] = code_table(digits, table, core, 0).astype(BF16)
    count = agg4.shape[1]
    agg = wide(agg4, 0, count)
    if len(state.shape) == 3:
        before = jnp.concatenate([state[source(k), 0:count, :] for k in range(CHANS)], axis=1).astype(F32)
    else:
        before = state[...]
    normed = rms(agg).astype(BF16)
    after = before + dot(normed, arrived((b0, b1, b2, b3), 0, agg.shape[1]))
    normed = rms(after.astype(BF16)).astype(BF16)

    def turned(weight):
        return jnp.concatenate([weight[columns_at(k), :] for k in range(CHANS)], axis=0)

    send[0:count, :] = dot(normed, turned(w_send)).astype(BF16)
    if has_recv:
        new_state[...] = after
        recv[...] = dot(normed, turned(w_recv)).astype(BF16)


def proc_kernel(pair, two, far, recv, inner, tab, agg):
    core = core_index()
    sib = 1 - core
    count = recv.shape[0]
    recv_t = transposed(recv[...])
    total = None
    for v, block in enumerate((two.at[core, 0], two.at[core, 1], pair.at[sib], far.at[sib])):
        lists = tab[v]
        total = add_edges(
            total, transposed(block[...]), recv_t, lists[0:1, :], lists[1:2, :], count, count
        )
    total = add_edges(total, transposed(pair[core]), recv_t, inner[0:1, :], inner[1:2, :], count, count)
    agg[...] = jnp.broadcast_to(total.T.astype(BF16)[None], agg.shape)


def dec_kernel(pair, two, far, latent, w_dd, dec_src, dec_dst, agg):
    core = core_index()
    recv_count = agg.shape[1]
    send_count = pair.shape[1] - 2 * TILE
    recv_t = dot(rms(latent[...]).astype(BF16), w_dd[...]).T.astype(BF16)
    arrivals = [(pair.at[core], dec_src[2:3, :], dec_dst[2:3, :])]
    for block, offset, second in places(pair, two, far, core):
        src, dst = [
            flat(decode(block[start : start + TILE, :], offset, second), 0, 4)
            for start in (send_count, send_count + TILE)
        ]
        arrivals.append((block, src, dst))
    total = None
    for block, src, dst in arrivals:
        total = add_edges(
            total, transposed(block[0:send_count, :]), recv_t, src, dst, send_count, recv_count
        )
    agg[...] = jnp.broadcast_to(total.T.astype(BF16)[None], agg.shape)


def out_kernel(agg4, latent, b0, b1, b2, b3, out):
    combined = jnp.concatenate(
        [agg4[source(k)].astype(F32) + latent[:, columns_at(k)].astype(F32) for k in range(CHANS)], axis=1
    )
    normed = rms(combined).astype(BF16)
    weights = arrived((b0, b1, b2, b3), 0, out.shape[0])
    out[...] = dot_last(weights, normed).astype(BF16)


def call(kernel, out_shapes, *args, scratch=()):
    return pl.pallas_call(
        kernel,
        out_shape=out_shapes,
        in_specs=[pl.BlockSpec(memory_space=pltpu.VMEM)] * len(args),
        out_specs=jax.tree.map(lambda _: pl.BlockSpec(memory_space=pltpu.VMEM), out_shapes),
        scratch_shapes=scratch,
        compiler_params=pltpu.CompilerParams(vmem_limit_bytes=16 * 1024 * 1024),
    )(*args)


def shape(dims, kind=BF16):
    return jax.ShapeDtypeStruct(dims, kind)


def exchange(copies):
    return lax.all_to_all(copies, "chan", 0, 0, tiled=True)


def core_gather(block):
    parts = lax.axis_size("band")
    return lax.all_gather(block, "band", axis_index_groups=[[s, s + 1] for s in range(0, parts, 2)])


def around(block):
    parts = lax.axis_size("band")
    pair = core_gather(block)
    sides = [[s, (s + 1) % parts] for s in range(1, parts, 2)]
    two = lax.all_gather(pair, "band", axis_index_groups=sides)
    near = jnp.where(core_index() == 0, two[0, 1], two[1, 0])
    return pair, two, core_gather(near)


def on_device(
    grid_state, mesh_latent, w_in, w_enc_src, w_enc_dst, w_enc_out, w_proc, w_dec_src, w_dec_dst, w_out,
    enc_src, enc_dst, local_src, local_dst, proc_src, proc_dst, dec_src, dec_dst,
):
    grid_count, channels = grid_state.shape
    mesh_count, width = mesh_latent.shape
    chans = lax.axis_size("chan")
    latent_width = width * chans

    channel_rows = -(-channels // LANES) * LANES
    late_rows = 3 * latent_width + channel_rows
    early = jnp.concatenate(
        [jnp.broadcast_to(part[None], (chans,) + part.shape) for part in (mesh_latent, w_in)], axis=1
    )
    early, w_enc_out = lax.optimization_barrier((early, w_enc_out))
    big = exchange(early)
    soon = (grid_state.T, w_enc_src, enc_src, enc_dst, proc_src, proc_dst)
    late = call(late_kernel, shape((late_rows, width)), w_enc_out, w_proc, w_out.T, *soon)
    blocks = [late] + [
        lax.ppermute(late, "chan", [(s, (s + k) % chans) for s in range(chans)]) for k in range(1, chans)
    ]

    payload, grid_latent = call(
        pre_kernel,
        (shape((grid_count + TABLES * TILE, width)), shape((grid_count, latent_width))),
        soon[0], big, *soon[1:],
        scratch=[pltpu.VMEM((16, enc_src.shape[1]), F32)],
    )
    pair, two, far = around(payload)
    agg, proc_tab, inner = call(
        enc_kernel,
        (
            shape((chans, mesh_count, width)),
            shape((4, 8, LANES), I32),
            shape((2, local_src.shape[1] + proc_src.shape[1]), I32),
        ),
        pair, two, far, big, w_enc_dst, enc_src, enc_dst, proc_src, proc_dst, local_src, local_dst,
    )
    agg, *blocks = lax.optimization_barrier((agg, *blocks))
    state = big
    for layer in range(w_proc.shape[0]):
        kernel = functools.partial(layer_kernel, layer)
        state, send, recv = call(
            functools.partial(later_kernel, kernel, layer * latent_width),
            (shape((mesh_count, latent_width), F32), shape((mesh_count, width)), shape((mesh_count, width))),
            exchange(agg), state, *blocks, w_proc,
        )
        pair, two, far = around(send)
        agg = call(
            proc_kernel, shape((chans, mesh_count, width)), pair, two, far, recv,
            inner, proc_tab,
        )
    node = functools.partial(later_kernel, functools.partial(node_kernel, False), 2 * latent_width)
    send = call(
        node, shape((mesh_count + 2 * TILE, width)),
        exchange(agg), state, *blocks, w_dec_src, dec_src, dec_dst,
        scratch=[pltpu.VMEM((16, dec_src.shape[1]), F32)],
    )
    pair, two, far = around(send)
    agg = call(
        dec_kernel, shape((chans, grid_count, width)), pair, two, far, grid_latent, w_dec_dst, dec_src, dec_dst
    )
    last = functools.partial(later_kernel, out_kernel, 3 * latent_width)
    return call(last, shape((channels, grid_count)), exchange(agg), grid_latent, *blocks).T


def solution(mesh):
    placed = (
        P("band", None),
        P("band", "chan"),
        P(None, "chan"),
        P(None, "chan"),
        P(None, "chan"),
        P(None, "chan"),
        P(None, None, None, "chan"),
        P(None, "chan"),
        P(None, "chan"),
        P("chan", None),
    ) + (P("band", None),) * 8
    return jax.shard_map(
        on_device, mesh=mesh, in_specs=placed, out_specs=P("band", None), check_vma=False
    )
```

```python
import functools

import jax
import jax.numpy as jnp
from jax import lax
from jax.experimental import pallas as pl
from jax.experimental.pallas import tpu as pltpu
from jax.sharding import PartitionSpec as P

EPS = 1e-05
F32 = jnp.float32
BF16 = jnp.bfloat16
I32 = jnp.int32
LANES = 128
CHANS = 4
TILE = 32
TABLES = 3


def rms(values):
    values = values.astype(F32)
    return values * lax.rsqrt(jnp.mean(values * values, axis=-1, keepdims=True) + EPS)


def silu(values):
    return 0.5 * values * (1.0 + jnp.tanh(0.5 * values))


def dot(a, b):
    return lax.dot_general(a, b, (((1,), (0,)), ((), ())), preferred_element_type=F32)


def dot_first(a, b):
    return lax.dot_general(a, b, (((0,), (0,)), ((), ())), preferred_element_type=F32)


def dot_last(a, b):
    return lax.dot_general(a, b, (((1,), (1,)), ((), ())), preferred_element_type=F32)


def flipped(weight, rows):
    return lax.dot_general(weight, rows, (((0,), (1,)), ((), ())), preferred_element_type=F32)


def wide(ref, start, size):
    return jnp.concatenate([ref[c, start : start + size, :] for c in range(ref.shape[0])], axis=1)


def core_index():
    return lax.axis_index("band") & 1


def one_hot(row, count):
    nodes = lax.broadcasted_iota(I32, (count, row.shape[1]), 0).astype(jnp.int16)
    hit = nodes == row.astype(jnp.int16)
    return jnp.where(hit, jnp.ones((), BF16), jnp.zeros((), BF16))


def code_table(digits, table, core, rows_used):
    width = table.shape[1]
    value = table[...] + 1
    digits[...] = jnp.zeros_like(digits)
    digits[0:5, 0:width] = (value >> 4).astype(F32)
    digits[8:13, 0:width] = (value & 15).astype(F32)
    row = lax.broadcasted_iota(I32, (TILE, 16), 0)
    col = lax.broadcasted_iota(I32, (TILE, 16), 1)
    near = row & 15
    base = jnp.where((row >> 4) == core, 3, 0)
    wanted = (near & 1) * 8 + base + ((near >> 1) & 1)
    total = None
    for k in range(width // LANES):
        pick = jnp.where((col == wanted) & ((near >> 2) == k + rows_used), 1.0, 0.0).astype(BF16)
        part = dot(pick, digits[:, k * LANES : (k + 1) * LANES].astype(BF16))
        total = part if total is None else total + part
    return total


def decode(tile, offset, second):
    row = lax.broadcasted_iota(I32, (8, TILE), 0)
    col = lax.broadcasted_iota(I32, (8, TILE), 1)
    place = offset + (row & 3) * 4 + second * 2
    weight = jnp.where(col == place, 16.0, jnp.where(col == place + 1, 1.0, 0.0))
    return dot(weight.astype(BF16), tile).astype(I32) - 1


def pre_kernel(
    grid_state, big, w_es, enc_src, enc_dst, proc_src, proc_dst, payload, latent, digits,
):
    core = core_index()
    channels, nodes = grid_state.shape
    first = big.shape[1] - channels
    grid_latent = silu(dot_first(grid_state[...], wide(big, first, channels))).astype(BF16)
    latent[...] = grid_latent
    payload[0:nodes, :] = dot(rms(grid_latent).astype(BF16), w_es[...]).astype(BF16)
    for t, table in enumerate((enc_src, enc_dst)):
        start = nodes + t * TILE
        payload[start : start + TILE, :] = code_table(digits, table, core, 0).astype(BF16)
    start = nodes + 2 * TILE
    both = code_table(digits, proc_src, core, 0) + code_table(digits, proc_dst, core, 1)
    payload[start : start + TILE, :] = both.astype(BF16)


def add_edges(total, send_t, recv_t, src, dst, send_count, recv_count):
    to = one_hot(dst, recv_count)
    ends = jnp.concatenate([one_hot(src, send_count), to], axis=0)
    message = silu(dot(jnp.concatenate([send_t, recv_t], axis=1), ends)).astype(BF16)
    part = dot_last(message, to)
    return part if total is None else total + part


def flat(rows, start, count):
    return jnp.concatenate([rows[start + k : start + k + 1, :] for k in range(count)], axis=1)


def places(pair, two, far, core):
    sib = 1 - core
    return (
        (two.at[core, 0], core * 16, 1),
        (two.at[core, 1], 16 - core * 16, 0),
        (pair.at[sib], 0, sib),
        (far.at[sib], 16, core),
    )


def transposed(values):
    return values.astype(F32).T.astype(BF16)


def enc_kernel(
    pair, two, far, big, w_ed, enc_src, enc_dst, proc_src, proc_dst, local_src, local_dst,
    agg, proc_tab, inner,
):
    core = core_index()
    recv_count = agg.shape[1]
    send_count = pair.shape[1] - TABLES * TILE
    count = local_src.shape[1]
    for i, (local, proc) in enumerate(((local_src, proc_src), (local_dst, proc_dst))):
        inner[i : i + 1, 0:count] = local[...]
        inner[i : i + 1, count:] = proc[2:3, :]
    recv = dot(rms(wide(big, 0, recv_count)).astype(BF16), w_ed[...])
    recv_t = recv.T.astype(BF16)
    arrivals = []
    for v, (block, offset, second) in enumerate(places(pair, two, far, core)):
        lists = [
            decode(block[send_count + t * TILE : send_count + (t + 1) * TILE, :], offset, second)
            for t in range(TABLES)
        ]
        arrivals.append((block, lists))
        proc_tab[v] = lists[2]
    total = None
    for block, lists in arrivals:
        total = add_edges(
            total, transposed(block[0:send_count, :]), recv_t, flat(lists[0], 0, 4), flat(lists[1], 0, 4),
            send_count, recv_count,
        )
    total = add_edges(
        total, transposed(pair[core, 0:send_count, :]), recv_t, enc_src[2:3, :], enc_dst[2:3, :],
        send_count, recv_count,
    )
    agg[...] = jnp.broadcast_to(total.T.astype(BF16)[None], agg.shape)


def source(k):
    return lax.rem(lax.axis_index("chan") + CHANS - k, CHANS)


def arrived(blocks, start, size):
    return jnp.concatenate([block[start : start + size, :] for block in blocks], axis=1)


def columns_at(k):
    return pl.ds(pl.multiple_of(source(k) * LANES, LANES), LANES)


class Rows:
    def __init__(self, ref, start):
        self.ref, self.start = ref, start

    def __getitem__(self, index):
        rows, columns = index
        return self.ref[self.start + rows.start : self.start + rows.stop, columns]


def later_kernel(kernel, start, agg4, state, b0, b1, b2, b3, *rest):
    kernel(agg4, state, *[Rows(b, start) for b in (b0, b1, b2, b3)], *rest)


def layer_kernel(layer, agg4, state, b0, b1, b2, b3, w_proc, *rest):
    node_kernel(True, agg4, state, b0, b1, b2, b3, w_proc.at[layer, 0], w_proc.at[layer, 1], *rest)


def late_kernel(w_enc_out, w_proc, w_out, *rest):
    out = rest[-1]
    depth = w_enc_out.shape[0]
    out[0:depth, :] = w_enc_out[...]
    out[depth : 2 * depth, :] = w_proc[0, 2]
    out[2 * depth : 3 * depth, :] = w_proc[1, 2]
    out[3 * depth : 3 * depth + w_out.shape[0], :] = w_out[...]


def node_kernel(has_recv, agg4, state, b0, b1, b2, b3, w_send, *rest):
    if has_recv:
        w_recv, new_state, send, recv = rest
    else:
        dec_src, dec_dst, send, digits = rest
        core = core_index()
        for t, table in enumerate((dec_src, dec_dst)):
            start = send.shape[0] - (2 - t) * TILE
            send[start : start + TILE, :] = code_table(digits, table, core, 0).astype(BF16)
    count = agg4.shape[1]
    agg = wide(agg4, 0, count)
    if len(state.shape) == 3:
        before = jnp.concatenate([state[source(k), 0:count, :] for k in range(CHANS)], axis=1).astype(F32)
    else:
        before = state[...]
    normed = rms(agg).astype(BF16)
    after = before + dot(normed, arrived((b0, b1, b2, b3), 0, agg.shape[1]))
    normed = rms(after.astype(BF16)).astype(BF16)

    def turned(weight):
        return jnp.concatenate([weight[columns_at(k), :] for k in range(CHANS)], axis=0)

    if has_recv:
        new_state[...] = after
        send[...] = flipped(turned(w_send), normed).astype(BF16)
        recv[...] = flipped(turned(w_recv), normed).astype(BF16)
    else:
        send[0:count, :] = dot(normed, turned(w_send)).astype(BF16)


def proc_kernel(pair, two, far, recv, inner, tab, agg):
    core = core_index()
    sib = 1 - core
    count = recv.shape[1]
    recv_t = recv[...]
    total = None
    for v, block in enumerate((two.at[core, 0], two.at[core, 1], pair.at[sib], far.at[sib])):
        lists = tab[v]
        total = add_edges(
            total, block[...], recv_t, lists[0:1, :], lists[1:2, :], count, count
        )
    total = add_edges(total, pair[core], recv_t, inner[0:1, :], inner[1:2, :], count, count)
    agg[...] = jnp.broadcast_to(total.T.astype(BF16)[None], agg.shape)


def dec_kernel(pair, two, far, latent, w_dd, dec_src, dec_dst, agg):
    core = core_index()
    recv_count = agg.shape[1]
    send_count = pair.shape[1] - 2 * TILE
    recv_t = dot(rms(latent[...]).astype(BF16), w_dd[...]).T.astype(BF16)
    arrivals = [(pair.at[core], dec_src[2:3, :], dec_dst[2:3, :])]
    for block, offset, second in places(pair, two, far, core):
        src, dst = [
            flat(decode(block[start : start + TILE, :], offset, second), 0, 4)
            for start in (send_count, send_count + TILE)
        ]
        arrivals.append((block, src, dst))
    total = None
    for block, src, dst in arrivals:
        total = add_edges(
            total, transposed(block[0:send_count, :]), recv_t, src, dst, send_count, recv_count
        )
    agg[...] = jnp.broadcast_to(total.T.astype(BF16)[None], agg.shape)


def out_kernel(agg4, latent, b0, b1, b2, b3, out):
    combined = jnp.concatenate(
        [agg4[source(k)].astype(F32) + latent[:, columns_at(k)].astype(F32) for k in range(CHANS)], axis=1
    )
    normed = rms(combined).astype(BF16)
    weights = arrived((b0, b1, b2, b3), 0, out.shape[0])
    out[...] = dot_last(weights, normed).astype(BF16)


def call(kernel, out_shapes, *args, scratch=()):
    return pl.pallas_call(
        kernel,
        out_shape=out_shapes,
        in_specs=[pl.BlockSpec(memory_space=pltpu.VMEM)] * len(args),
        out_specs=jax.tree.map(lambda _: pl.BlockSpec(memory_space=pltpu.VMEM), out_shapes),
        scratch_shapes=scratch,
        compiler_params=pltpu.CompilerParams(vmem_limit_bytes=16 * 1024 * 1024),
    )(*args)


def shape(dims, kind=BF16):
    return jax.ShapeDtypeStruct(dims, kind)


def exchange(copies):
    return lax.all_to_all(copies, "chan", 0, 0, tiled=True)


def core_gather(block):
    parts = lax.axis_size("band")
    return lax.all_gather(block, "band", axis_index_groups=[[s, s + 1] for s in range(0, parts, 2)])


def around(block):
    parts = lax.axis_size("band")
    pair = core_gather(block)
    sides = [[s, (s + 1) % parts] for s in range(1, parts, 2)]
    two = lax.all_gather(pair, "band", axis_index_groups=sides)
    near = jnp.where(core_index() == 0, two[0, 1], two[1, 0])
    return pair, two, core_gather(near)


def on_device(
    grid_state, mesh_latent, w_in, w_enc_src, w_enc_dst, w_enc_out, w_proc, w_dec_src, w_dec_dst, w_out,
    enc_src, enc_dst, local_src, local_dst, proc_src, proc_dst, dec_src, dec_dst,
):
    grid_count, channels = grid_state.shape
    mesh_count, width = mesh_latent.shape
    chans = lax.axis_size("chan")
    latent_width = width * chans

    channel_rows = -(-channels // LANES) * LANES
    late_rows = 3 * latent_width + channel_rows
    early = jnp.concatenate(
        [jnp.broadcast_to(part[None], (chans,) + part.shape) for part in (mesh_latent, w_in)], axis=1
    )
    early, w_enc_out = lax.optimization_barrier((early, w_enc_out))
    big = exchange(early)
    soon = (grid_state.T, w_enc_src, enc_src, enc_dst, proc_src, proc_dst)
    late = call(late_kernel, shape((late_rows, width)), w_enc_out, w_proc, w_out.T, *soon)
    blocks = [late] + [
        lax.ppermute(late, "chan", [(s, (s + k) % chans) for s in range(chans)]) for k in range(1, chans)
    ]

    payload, grid_latent = call(
        pre_kernel,
        (shape((grid_count + TABLES * TILE, width)), shape((grid_count, latent_width))),
        soon[0], big, *soon[1:],
        scratch=[pltpu.VMEM((16, enc_src.shape[1]), F32)],
    )
    pair, two, far = around(payload)
    agg, proc_tab, inner = call(
        enc_kernel,
        (
            shape((chans, mesh_count, width)),
            shape((4, 8, LANES), I32),
            shape((2, local_src.shape[1] + proc_src.shape[1]), I32),
        ),
        pair, two, far, big, w_enc_dst, enc_src, enc_dst, proc_src, proc_dst, local_src, local_dst,
    )
    agg, *blocks = lax.optimization_barrier((agg, *blocks))
    state = big
    for layer in range(w_proc.shape[0]):
        kernel = functools.partial(layer_kernel, layer)
        state, send, recv = call(
            functools.partial(later_kernel, kernel, layer * latent_width),
            (shape((mesh_count, latent_width), F32), shape((width, mesh_count)), shape((width, mesh_count))),
            exchange(agg), state, *blocks, w_proc,
        )
        pair, two, far = around(send)
        agg = call(
            proc_kernel, shape((chans, mesh_count, width)), pair, two, far, recv,
            inner, proc_tab,
        )
    node = functools.partial(later_kernel, functools.partial(node_kernel, False), 2 * latent_width)
    send = call(
        node, shape((mesh_count + 2 * TILE, width)),
        exchange(agg), state, *blocks, w_dec_src, dec_src, dec_dst,
        scratch=[pltpu.VMEM((16, dec_src.shape[1]), F32)],
    )
    pair, two, far = around(send)
    agg = call(
        dec_kernel, shape((chans, grid_count, width)), pair, two, far, grid_latent, w_dec_dst, dec_src, dec_dst
    )
    last = functools.partial(later_kernel, out_kernel, 3 * latent_width)
    return call(last, shape((channels, grid_count)), exchange(agg), grid_latent, *blocks).T


def solution(mesh):
    placed = (
        P("band", None),
        P("band", "chan"),
        P(None, "chan"),
        P(None, "chan"),
        P(None, "chan"),
        P(None, "chan"),
        P(None, None, None, "chan"),
        P(None, "chan"),
        P(None, "chan"),
        P("chan", None),
    ) + (P("band", None),) * 8
    return jax.shard_map(
        on_device, mesh=mesh, in_specs=placed, out_specs=P("band", None), check_vma=False
    )
```
